32 devices in a mesh: fsdp: 4 (over y, x), ctx: 8 (over z, core).
Axes of the slice: x: 2, y: 2, z: 4, core: 2. Of those that a mesh axis runs over, the one named last changes fastest.
Arguments:
- inputs: bfloat16 [4, 1024, 2048], P('fsdp', 'ctx'), may hold values from -6 to 6
- queries: bfloat16 [4, 1024, 3072], P('fsdp', 'ctx'), may hold values from -210 to 210
- kv_down: bfloat16 [2048, 576], replicated, may hold values from -0.125 to 0.125
- latent_gain: bfloat16 [512], replicated, may hold values from 0.25 to 1.75
- kv_up: bfloat16 [512, 4096], replicated, may hold values from -0.25 to 0.25
- out_proj: bfloat16 [2048, 2048], replicated, may hold values from -0.125 to 0.125
- post_gain: bfloat16 [2048], replicated, may hold values from 0.25 to 1.75
- expert_ids: int32 [4, 1024, 6], P('fsdp', 'ctx'), may hold values from 0 to 15, all different within a row; in each aligned block of 128 rows (0 to 127, 128 to 255, ..., all dimensions but the last counted through in order) at most 96 rows name the same one
- gates: float32 [4, 1024, 6], P('fsdp', 'ctx'), may hold values from 0.1 to 1
- gate_up: bfloat16 [16, 2048, 1536], P('ctx', 'fsdp'), may hold values from -0.125 to 0.125
- down_proj: bfloat16 [16, 2048, 768], P('ctx', 'fsdp'), may hold values from -0.21875 to 0.21875
Outputs:
- attn_out: bfloat16 [4, 1024, 2048], P('fsdp', 'ctx')
- moe_out: bfloat16 [4, 1024, 2048], P('fsdp', 'ctx')
The draws below stay inside these ranges and needn't reach their ends.
Inputs may be any that keep to these rules, and one draw needn't show every extreme that they name: `expert_ids`: within the 128 consecutive positions of a sequence on one index of ctx, no expert is chosen by more than 96 picks, a bound that some block reaches. The 6 experts of a token differ.
All inputs are finite; a program needn't handle non-finite values.
Results may differ from the reference program's by a relative error of at most 0.02.
The reference program's roundings to bfloat16 on the way count: a program that leaves them out, or rounds other values in their place, can miss the bound.
Values may be sent and summed in bfloat16 or wider, within the bound.
No kernel may reach another device: no remote copies, remote signals or barrier semaphores. Data moves between devices by JAX's collectives and lax.ppermute only.
A program may use at most 192 MiB of HBM per device.

```python
import math
import jax
import jax.numpy as jnp
import numpy as np
from jax import lax

D = 2048
HEADS = 16
NOPE = 128
ROPE = 64
VDIM = 128
KVL = 512
FFE = 768
TOP = 6
S_DEV = 128
EXPERTS = 16
SEQ = 1024
SEQS = 4
CAP = 96


def draw_queries(key, part):
    shape = (SEQS, SEQ, HEADS * (NOPE + ROPE))
    first = jax.random.fold_in(key, 11)
    values = jnp.clip(jax.random.normal(first, shape, jnp.float32), -6.0, 6.0)
    return values.astype(jnp.bfloat16)


def level_of(stream_key, shape, shards, smallest, high):
    def one(position, shards_of):
        steps = jax.random.uniform(jax.random.fold_in(jax.random.fold_in(stream_key, 6), position), (shards_of,), jnp.float32, smallest / len(shards), high / len(shards))
        return jnp.repeat(jnp.exp(steps), shape[position] // shards_of).reshape((-1,) + (1,) * (len(shape) - position - 1))

    level = one(*shards[0])
    for cut in shards[1:]:
        level = level * one(*cut)
    return level


def shared_out(key, own, number, rows, amount, top, limit, slope):
    order = jax.random.permutation(key, amount)
    heavy_load, common = load_shares(amount, rows * top, limit, slope, True), load_shares(amount, rows * top, limit, slope, False)
    places = jnp.arange(amount)

    def named(lengths, turn):
        used = int((lengths > 0).sum())
        fixed = max(1, used // 4)
        passed = fixed + (places - fixed + turn * (used - fixed)) % max(1, amount - fixed)
        return jnp.zeros((amount,), jnp.int32).at[order[jnp.where(places < fixed, places, passed)]].set(jnp.asarray(lengths, jnp.int32))

    lengths = jnp.where(number % 4 == 0, named(heavy_load, number // 4), named(common, number - number // 4 - 1))
    mixed = jax.random.permutation(jax.random.fold_in(own, 3), amount)
    giver, sink = mixed[0:amount // 2 * 2:2], mixed[1:amount // 2 * 2:2]
    slack = jnp.minimum(lengths[giver] - 1, limit - lengths[sink]) // 2
    slack = jnp.where((giver == order[0]) | (sink == order[0]) | (lengths[sink] == 0), 0, jnp.maximum(slack, 0))
    passed = jax.random.randint(jax.random.fold_in(own, 4), (amount // 2,), 0, 1 << 20) % (slack + 1)
    lengths = lengths.at[giver].add(-passed).at[sink].add(passed)
    items = jnp.searchsorted(jnp.cumsum(lengths), jnp.arange(rows * top), side="right").astype(jnp.int32)
    grid = items.reshape(top, rows).T
    grid = grid[jax.random.permutation(jax.random.fold_in(own, 1), rows)]
    turn = jax.random.randint(jax.random.fold_in(own, 2), (rows, 1), 0, top)
    return jnp.take_along_axis(grid, (jnp.arange(top)[None, :] + turn) % top, axis=1)


def load_shares(amount, total, most, lean, full):
    portions = [(1 << 20) // math.isqrt(standing ** lean) + 1 for standing in range(1, amount + 1)]
    largest = most if full else min(most, max(-(-total // amount), total * portions[0] // sum(portions)))
    least = 1 if total - largest >= amount - 1 else 0
    holding, rest = [largest] + [least] * (amount - 1), total - largest - least * (amount - 1)
    while rest > 0:
        candidates = [i for i in range(1, amount) if holding[i] < largest] or [i for i in range(1, amount) if holding[i] < most]
        mass, remaining = sum([portions[i] for i in candidates]), rest
        for i in candidates:
            more = min(most - holding[i], max(1, remaining * portions[i] // mass), rest)
            holding[i] = holding[i] + more
            rest = rest - more
    return np.array(holding)


def centred(key, shape, spread, limit, pieces=(), dtype=jnp.bfloat16):
    values = jax.random.normal(key, shape, jnp.float32) * spread
    if len(pieces) > 0:
        values = level_of(key, shape, pieces, -0.22, 0.18) * values
    return jnp.clip(values, min=-limit, max=limit).astype(dtype)


def setup_inputs(seed: int = 0) -> dict:
    splits = jax.random.split(jax.random.key(seed), 12)
    inputs = centred(splits[0], (SEQS, SEQ, D), 1.0, 6.0, ((0, 4), (1, 8)))
    queries = draw_queries(jax.random.fold_in(splits[11], 71), 0)
    kv_down = centred(splits[2], (D, KVL + ROPE), D ** -0.5, 0.125)
    latent_gain = jnp.clip(1.0 + 0.15 * jax.random.normal(splits[3], (KVL,), jnp.float32), 0.25, 1.75).astype(jnp.bfloat16)
    kv_up = centred(splits[4], (KVL, HEADS * (NOPE + VDIM)), KVL ** -0.5, 0.25)
    out_proj = centred(splits[5], (HEADS * VDIM, D), (HEADS * VDIM) ** -0.5, 0.125)
    post_gain = jnp.clip(1.0 + 0.15 * jax.random.normal(splits[6], (D,), jnp.float32), 0.25, 1.75).astype(jnp.bfloat16)
    expert_ids_keys = jax.random.split(jax.random.fold_in(splits[7], 1), SEQS * SEQ // S_DEV)
    expert_ids_turns = jax.random.permutation(jax.random.fold_in(splits[7], 3), SEQS * SEQ // S_DEV)
    expert_ids = jax.vmap(lambda own, number: shared_out(jax.random.fold_in(splits[7], 2), own, number, S_DEV, EXPERTS, TOP, CAP, 2))(expert_ids_keys, expert_ids_turns).reshape((SEQS, SEQ, TOP))
    gates = jnp.clip(0.1 + 0.9 * jax.random.uniform(splits[8], (SEQS, SEQ, TOP), jnp.float32) ** level_of(splits[8], (SEQS, SEQ, TOP), ((0, 4), (1, 8)), -0.2, 0.2), 0.1, 1.0)
    gate_up = centred(splits[9], (EXPERTS, D, 2 * FFE), D ** -0.5, 0.125, ((0, 8), (1, 4)))
    down_proj = centred(splits[10], (EXPERTS, D, FFE), FFE ** -0.5, 0.21875, ((0, 8), (1, 4)))
    return {"inputs": inputs, "queries": queries, "kv_down": kv_down, "latent_gain": latent_gain, "kv_up": kv_up, "out_proj": out_proj, "post_gain": post_gain, "expert_ids": expert_ids, "gates": gates, "gate_up": gate_up, "down_proj": down_proj}


EPSILON = 1e-06
NEG_LARGE = -1e+30

def normalize(values, gain):
    mean_sq = lax.optimization_barrier(jnp.mean(values * values, axis=-1, keepdims=True))
    return values * lax.rsqrt(mean_sq + EPSILON) * gain.astype(jnp.float32)

def rotate(values, angles):
    half = values.shape[-1] // 2
    first = values[..., :half]
    second = values[..., half:]
    cosine = jnp.cos(angles)
    sine = jnp.sin(angles)
    return jnp.concatenate([first * cosine - second * sine, second * cosine + first * sine], axis=-1)

def angles_of(positions, width):
    half = width // 2
    freqs = jnp.exp(-(2.0 * jnp.arange(half).astype(jnp.float32) / width) * math.log(10000.0))
    return positions.astype(jnp.float32)[:, None] * freqs[None, :]

def rounded(values):
    return lax.optimization_barrier(values.astype(jnp.bfloat16))

def reference(inputs, queries, kv_down, latent_gain, kv_up, out_proj, post_gain, expert_ids, gates, gate_up, down_proj):
    up_heads = kv_up.reshape(KVL, HEADS, NOPE + VDIM)
    key_part = up_heads[:, :, :NOPE].astype(jnp.float32)
    value_part = up_heads[:, :, NOPE:].astype(jnp.float32)

    def one_sequence(pair):
        tokens, query_rows = pair
        positions = jnp.arange(SEQ).astype(jnp.int32)
        angles = angles_of(positions, ROPE)
        compressed = jnp.dot(tokens, kv_down, preferred_element_type=jnp.float32)
        latent = normalize(compressed[:, :KVL], latent_gain)
        key_rope = rotate(compressed[:, KVL:], angles)
        cache = rounded(jnp.concatenate([latent, key_rope], axis=1))
        query_heads = query_rows.reshape(SEQ, HEADS, NOPE + ROPE)
        absorbed = jnp.einsum('thn,lhn->thl', query_heads[:, :, :NOPE].astype(jnp.float32), key_part)
        query_rope = rotate(query_heads[:, :, NOPE:].astype(jnp.float32), angles[:, None, :])
        scale = (NOPE + ROPE) ** (-0.5)
        packed = rounded(jnp.concatenate([absorbed, query_rope], axis=2) * scale)
        cache_wide = cache.astype(jnp.float32)
        scores = jnp.einsum('thc,uc->htu', packed.astype(jnp.float32), cache_wide)
        allowed = (positions[None, :] <= positions[:, None])[None, :, :]
        scores = jnp.where(allowed, scores, NEG_LARGE)
        peak = lax.optimization_barrier(jnp.max(scores, axis=2, keepdims=True))
        expo = jnp.where(allowed, jnp.exp(scores - peak), 0.0)
        total = lax.optimization_barrier(jnp.sum(expo, axis=2))
        weights = rounded(expo).astype(jnp.float32)
        context = jnp.einsum('htu,ul->thl', weights, cache_wide[:, :KVL])
        context = rounded(context / jnp.transpose(total)[:, :, None])
        heads = jnp.einsum('thl,lhv->thv', context.astype(jnp.float32), value_part)
        heads = heads.astype(jnp.bfloat16).reshape(SEQ, HEADS * VDIM)
        attn = jnp.dot(heads, out_proj, preferred_element_type=jnp.float32)
        routed = normalize(tokens.astype(jnp.float32) + attn, post_gain).astype(jnp.bfloat16)
        return (attn.astype(jnp.bfloat16), routed)
    attn_out, routed_in = lax.map(one_sequence, (inputs, queries))
    count = SEQS * SEQ
    routed_flat = routed_in.reshape(count, D)
    blocks = count // S_DEV
    picks = expert_ids.reshape(blocks, S_DEV * TOP)
    onehot = (picks[:, :, None] == jnp.arange(EXPERTS).astype(jnp.int32)[None, None, :]).astype(jnp.int32)
    before = jnp.cumsum(onehot, axis=1) - onehot
    slot = lax.optimization_barrier(jnp.sum(before * onehot, axis=2))
    block_index = jnp.arange(blocks).astype(jnp.int32)[:, None]
    target = (picks * (blocks * CAP) + block_index * CAP + slot).reshape(-1)
    owner = (jnp.arange(count * TOP) // TOP).astype(jnp.int32)
    table = jnp.zeros((EXPERTS * blocks * CAP,), jnp.int32).at[target].set(owner).reshape(EXPERTS, blocks * CAP)
    weight_table = jnp.zeros((EXPERTS * blocks * CAP,), jnp.float32).at[target].set(gates.reshape(-1)).reshape(EXPERTS, blocks * CAP)

    def add_expert(running, index):
        rows_index = table[index]
        rows = routed_flat[rows_index]
        joint = jnp.dot(rows, gate_up[index], preferred_element_type=jnp.float32)
        hidden = (jax.nn.silu(joint[:, :FFE]) * joint[:, FFE:]).astype(jnp.bfloat16)
        result = jnp.dot(hidden, jnp.transpose(down_proj[index]), preferred_element_type=jnp.float32)
        result = rounded(result).astype(jnp.float32)
        running = running.at[rows_index].add(weight_table[index][:, None] * result)
        return (running, None)
    summed, unused = lax.scan(add_expert, jnp.zeros((count, D), jnp.float32), jnp.arange(EXPERTS).astype(jnp.int32))
    moe_out = summed.astype(jnp.bfloat16).reshape(SEQS, SEQ, D)
    return (attn_out, moe_out)
```

```python
import functools
import math

import jax
import jax.numpy as jnp
from jax import lax
from jax.experimental import pallas as pl
from jax.experimental.pallas import tpu as pltpu
from jax.sharding import PartitionSpec as P

HEADS = 16
NOPE = 128
ROPE = 64
VDIM = 128


EPSILON = 1e-06
NEG_LARGE = -1e30
CORES = 2


def normalize(values, gain):
    mean_sq = jnp.mean(values * values, axis=-1, keepdims=True)
    return values * lax.rsqrt(mean_sq + EPSILON) * gain.astype(jnp.float32)


def rotate(values, angles):
    half = values.shape[-1] // 2
    first = values[..., :half]
    second = values[..., half:]
    cosine = jnp.cos(angles)
    sine = jnp.sin(angles)
    return jnp.concatenate(
        [first * cosine - second * sine, second * cosine + first * sine], axis=-1
    )


def angles_of(positions, width):
    half = width // 2
    freqs = jnp.exp(-(2.0 * jnp.arange(half, dtype=jnp.float32) / width) * math.log(10000.0))
    return positions.astype(jnp.float32)[:, None] * freqs[None, :]


def flip(values, axis, mask):
    size = lax.axis_size(axis)
    return lax.ppermute(values, axis, [(i, i ^ mask) for i in range(size)])


def turn(values, step):
    size = lax.axis_size("ctx")
    return lax.ppermute(values, "ctx", [(i, (i + CORES * step) % size) for i in range(size)])


def gather_pieces(shard):
    size = lax.axis_size("fsdp")
    if size == 4:
        half = shard.shape[0] // 2
        by_one = flip(shard, "fsdp", 1)
        by_two = flip(shard, "fsdp", 2)
        low = flip(by_one[:half], "fsdp", 2)
        high = flip(by_two[half:], "fsdp", 1)
        return {0: [shard], 1: [by_one], 2: [by_two], 3: [low, high]}
    pieces = {0: [shard]}
    bit = 1
    while bit < size:
        for offset in list(pieces):
            pieces[offset | bit] = [flip(pieces[offset][0], "fsdp", bit)]
        bit *= 2
    return pieces


def gather_blocks(block):
    turns = lax.axis_size("ctx") // CORES
    mine = [block] + [turn(block, d) for d in range(1, turns)]
    mine = jnp.stack(mine)
    other = flip(mine, "ctx", 1)
    return mine, other


def up_kernel(offsets, depth, index_ref, x_ref, gate_ref, *refs):
    out_ref = refs[-1]
    weights = refs[:-1]
    me = index_ref[0]
    joint = None
    for offset, weight in zip(offsets, weights):
        start = pl.multiple_of(jnp.bitwise_xor(me, offset) * depth, depth)
        term = jnp.dot(
            x_ref[:, pl.ds(start, depth)], weight[0], preferred_element_type=jnp.float32
        )
        joint = term if joint is None else joint + term
    width = out_ref.shape[1]
    value = joint[:, :width]
    hidden = value / (1.0 + jnp.exp(-value)) * joint[:, width:]
    out_ref[...] = (hidden * gate_ref[...]).astype(jnp.bfloat16)


def up(index, tokens, gate, expert, pieces):
    rows, width_model = tokens.shape
    offsets = sorted(pieces)
    operands, specs = [], []
    depth = pieces[0][0].shape[1]
    joint_width = pieces[0][0].shape[2]
    for offset in offsets:
        parts = pieces[offset]
        per = parts[0].shape[0]
        operands.append(parts[expert // per])
        specs.append(
            pl.BlockSpec((1, depth, joint_width), lambda r, s, at=expert % per: (at, 0, 0))
        )
    tile = 256
    return pl.pallas_call(
        functools.partial(up_kernel, offsets, depth),
        grid_spec=pltpu.PrefetchScalarGridSpec(
            num_scalar_prefetch=1,
            grid=(rows // tile,),
            in_specs=[
                pl.BlockSpec((tile, width_model), lambda r, s: (r, 0)),
                pl.BlockSpec((tile, 1), lambda r, s: (r, 0)),
            ]
            + specs,
            out_specs=pl.BlockSpec((tile, joint_width // 2), lambda r, s: (r, 0)),
        ),
        out_shape=jax.ShapeDtypeStruct((rows, joint_width // 2), jnp.bfloat16),
        compiler_params=pltpu.CompilerParams(vmem_limit_bytes=48 * 2**20),
        cost_estimate=pl.CostEstimate(
            flops=2 * rows * width_model * joint_width,
            bytes_accessed=2 * (rows * width_model + width_model * joint_width),
            transcendentals=0,
        ),
    )(index, tokens, gate, *operands)


def down_kernel(h0_ref, h1_ref, w0_ref, w1_ref, out_ref):
    nt = (((1,), (1,)), ((), ()))
    out = lax.dot_general(h0_ref[...], w0_ref[0], nt, preferred_element_type=jnp.float32)
    out += lax.dot_general(h1_ref[...], w1_ref[0], nt, preferred_element_type=jnp.float32)
    out_ref[...] = out.astype(jnp.bfloat16)


def down(hidden, parts):
    rows, width = hidden[0].shape
    per = parts[0].shape[0]
    depth = parts[0].shape[1]
    tile = 256
    spec_h = pl.BlockSpec((tile, width), lambda r: (r, 0))

    def spec_w(expert):
        return pl.BlockSpec((1, depth, width), lambda r, at=expert % per: (at, 0, 0))

    return pl.pallas_call(
        down_kernel,
        grid=(rows // tile,),
        in_specs=[spec_h, spec_h, spec_w(0), spec_w(1)],
        out_specs=pl.BlockSpec((tile, depth), lambda r: (r, 0)),
        out_shape=jax.ShapeDtypeStruct((rows, depth), jnp.bfloat16),
        compiler_params=pltpu.CompilerParams(vmem_limit_bytes=48 * 2**20),
        cost_estimate=pl.CostEstimate(
            flops=4 * rows * width * depth,
            bytes_accessed=4 * (rows + depth) * width + 2 * rows * depth,
            transcendentals=0,
        ),
    )(hidden[0], hidden[1], parts[0], parts[1 // per])


def return_blocks(partial, rows):
    turns = lax.axis_size("ctx") // CORES
    count = turns * rows
    arrived = flip(partial[count:], "ctx", 1)
    both = partial[:count].astype(jnp.float32) + arrived.astype(jnp.float32)
    sent = both[rows:].astype(jnp.bfloat16)
    total = both[:rows]
    for d in range(1, turns):
        total += turn(sent[(d - 1) * rows : d * rows], turns - d).astype(jnp.float32)
    return total.astype(jnp.bfloat16)


def per_device(
    inputs,
    queries,
    kv_down,
    latent_gain,
    kv_up,
    out_proj,
    post_gain,
    expert_ids,
    gates,
    gate_up,
    down_proj,
):
    tokens = inputs[0]
    rows = tokens.shape[0]
    width_model = tokens.shape[1]
    ctx_size = lax.axis_size("ctx")
    rank = lax.axis_index("ctx")
    here = lax.axis_index("fsdp")
    turns = ctx_size // CORES
    local_experts = gate_up.shape[0]
    experts = local_experts * ctx_size

    up_pieces = gather_pieces(gate_up)
    down_pieces = gather_pieces(down_proj)

    row_iota = jnp.arange(rows, dtype=jnp.int32)
    positions = rank * rows + row_iota
    angles = angles_of(positions, ROPE)
    latent_width = latent_gain.shape[0]
    compressed = jnp.dot(tokens, kv_down, preferred_element_type=jnp.float32)
    latent = normalize(compressed[:, :latent_width], latent_gain)
    key_rope = rotate(compressed[:, latent_width:], angles)

    chosen = expert_ids[0][:, :, None] == jnp.arange(experts, dtype=jnp.int32)
    table = jnp.sum(jnp.where(chosen, gates[0][:, :, None], 0.0), axis=1)
    table_high = table.astype(jnp.bfloat16)
    table_low = (table - table_high.astype(jnp.float32)).astype(jnp.bfloat16)
    cache = jnp.concatenate(
        [latent.astype(jnp.bfloat16), key_rope.astype(jnp.bfloat16), table_high, table_low], axis=1
    )
    mine, other = gather_blocks(cache)
    every = jnp.concatenate([mine, other]).reshape(ctx_size * rows, cache.shape[1])
    key_width = latent_width + ROPE
    keys = every[:, :key_width]
    z = rank // CORES
    core = rank % CORES
    owners = jnp.concatenate(
        [
            jnp.stack([((z - d) % turns) * CORES + core for d in range(turns)]),
            jnp.stack([((z - d) % turns) * CORES + 1 - core for d in range(turns)]),
        ]
    )
    key_pos = (owners[:, None] * rows + row_iota[None, :]).reshape(-1)
    table_all = every[:, key_width:].astype(jnp.float32)
    table_all = table_all[:, :experts] + table_all[:, experts : 2 * experts]
    gate_columns = lax.dynamic_slice(
        table_all, (0, rank * local_experts), (ctx_size * rows, local_experts)
    )

    up_heads = kv_up.reshape(latent_width, HEADS, NOPE + VDIM)
    scale = (NOPE + ROPE) ** (-0.5)
    query_heads = queries[0].reshape(rows, HEADS, NOPE + ROPE)
    absorbed = jnp.einsum(
        "thn,lhn->htl",
        query_heads[:, :, :NOPE],
        up_heads[:, :, :NOPE],
        preferred_element_type=jnp.float32,
    )
    query_rope = rotate(query_heads[:, :, NOPE:].astype(jnp.float32), angles[:, None, :])
    query_rope = jnp.transpose(query_rope, (1, 0, 2))
    packed = (jnp.concatenate([absorbed, query_rope], axis=2) * scale).astype(jnp.bfloat16)
    packed = packed.reshape(HEADS * rows, key_width)
    row_pos = jnp.tile(positions, HEADS)
    scores = jnp.dot(packed, keys.T, preferred_element_type=jnp.float32)
    allowed = key_pos[None, :] <= row_pos[:, None]
    scores = jnp.where(allowed, scores, NEG_LARGE)
    peak = jnp.max(scores, axis=1, keepdims=True)
    expo = jnp.exp(scores - peak)
    total = jnp.sum(expo, axis=1)
    acc = jnp.dot(
        expo.astype(jnp.bfloat16), keys[:, :latent_width], preferred_element_type=jnp.float32
    )
    context = (acc / total[:, None]).astype(jnp.bfloat16).reshape(HEADS, rows, latent_width)
    heads = jnp.einsum(
        "htl,lhv->thv", context, up_heads[:, :, NOPE:], preferred_element_type=jnp.float32
    )
    heads = heads.astype(jnp.bfloat16).reshape(rows, HEADS * VDIM)
    attn = jnp.dot(heads, out_proj, preferred_element_type=jnp.float32)
    attn_out = attn.astype(jnp.bfloat16)
    routed_in = normalize(tokens.astype(jnp.float32) + attn, post_gain).astype(jnp.bfloat16)

    mine, other = gather_blocks(routed_in)
    routed = jnp.concatenate([mine, other]).reshape(ctx_size * rows, width_model)
    index = jnp.reshape(here, (1,)).astype(jnp.int32)
    hidden = [
        up(index, routed, gate_columns[:, e : e + 1], e, up_pieces) for e in range(local_experts)
    ]
    depth = down_proj.shape[1]
    moe = jnp.zeros((rows, width_model), jnp.bfloat16)
    for offset in sorted(down_pieces):
        partial = down(hidden, down_pieces[offset])
        owned = return_blocks(partial, rows)
        moe = lax.dynamic_update_slice(moe, owned, (0, jnp.bitwise_xor(here, offset) * depth))
    return (attn_out[None], moe[None])


def solution(mesh):
    in_specs = (
        P("fsdp", "ctx", None),
        P("fsdp", "ctx", None),
        P(),
        P(),
        P(),
        P(),
        P(),
        P("fsdp", "ctx", None),
        P("fsdp", "ctx", None),
        P("ctx", "fsdp", None),
        P("ctx", "fsdp", None),
    )
    out_specs = (P("fsdp", "ctx", None), P("fsdp", "ctx", None))
    return jax.shard_map(
        per_device, mesh=mesh, in_specs=in_specs, out_specs=out_specs, check_vma=False
    )
```

```python
import functools
import math

import jax
import jax.numpy as jnp
from jax import lax
from jax.experimental import pallas as pl
from jax.experimental.pallas import tpu as pltpu
from jax.sharding import PartitionSpec as P

HEADS = 16
NOPE = 128
ROPE = 64
VDIM = 128


EPSILON = 1e-06
NEG_LARGE = -1e30
CORES = 2


def normalize(values, gain):
    mean_sq = jnp.mean(values * values, axis=-1, keepdims=True)
    return values * lax.rsqrt(mean_sq + EPSILON) * gain.astype(jnp.float32)


def rotate(values, angles):
    half = values.shape[-1] // 2
    first = values[..., :half]
    second = values[..., half:]
    cosine = jnp.cos(angles)
    sine = jnp.sin(angles)
    return jnp.concatenate(
        [first * cosine - second * sine, second * cosine + first * sine], axis=-1
    )


def angles_of(positions, width):
    half = width // 2
    freqs = jnp.exp(-(2.0 * jnp.arange(half, dtype=jnp.float32) / width) * math.log(10000.0))
    return positions.astype(jnp.float32)[:, None] * freqs[None, :]


def flip(values, axis, mask):
    size = lax.axis_size(axis)
    return lax.ppermute(values, axis, [(i, i ^ mask) for i in range(size)])


def turn(values, step):
    size = lax.axis_size("ctx")
    return lax.ppermute(values, "ctx", [(i, (i + CORES * step) % size) for i in range(size)])


def after(value, *earlier):
    return lax.optimization_barrier((value, *earlier))[0]


def first_step(shard):
    return {0: [shard], 1: [flip(shard, "fsdp", 1)], 2: [flip(shard, "fsdp", 2)]}


def second_step(pieces):
    size = lax.axis_size("fsdp")
    half = pieces[0][0].shape[0] // 2
    if size == 4:
        low = flip(pieces[1][0][:half], "fsdp", 2)
        high = flip(pieces[2][0][half:], "fsdp", 1)
        return {3: [low, high]}
    more = {3: [flip(pieces[1][0], "fsdp", 2)]}
    held = {**pieces, **more}
    bit = 4
    while bit < size:
        new = {o | bit: [flip(p[0], "fsdp", bit)] for o, p in held.items()}
        more.update(new)
        held.update(new)
        bit *= 2
    return more


def gather_blocks(block, *earlier):
    turns = lax.axis_size("ctx") // CORES
    near = [d for d in range(1, turns) if d in (1, turns - 1)]
    arrived = {0: block}
    for d in near:
        arrived[d] = turn(block, d)
    late = after(block, *earlier) if earlier else block
    for d in range(1, turns):
        if d not in near:
            arrived[d] = turn(late, d)
    mine = jnp.stack([arrived[d] for d in range(turns)])
    other = flip(mine, "ctx", 1)
    return mine, other


def up_kernel(offsets, depth, index_ref, x_ref, gate_ref, *refs):
    out_ref = refs[-1]
    weights = refs[:-1]
    me = index_ref[0]
    joint = None
    for offset, weight in zip(offsets, weights):
        start = pl.multiple_of(jnp.bitwise_xor(me, offset) * depth, depth)
        term = jnp.dot(
            x_ref[:, pl.ds(start, depth)], weight[0], preferred_element_type=jnp.float32
        )
        joint = term if joint is None else joint + term
    width = out_ref.shape[1]
    value = joint[:, :width]
    hidden = value / (1.0 + jnp.exp(-value)) * joint[:, width:]
    out_ref[...] = (hidden * gate_ref[...]).astype(jnp.bfloat16)


def up(index, tokens, gate, expert, pieces):
    rows, width_model = tokens.shape
    offsets = sorted(pieces)
    operands, specs = [], []
    depth = pieces[0][0].shape[1]
    joint_width = pieces[0][0].shape[2]
    for offset in offsets:
        parts = pieces[offset]
        per = parts[0].shape[0]
        operands.append(parts[expert // per])
        specs.append(
            pl.BlockSpec((1, depth, joint_width), lambda r, s, at=expert % per: (at, 0, 0))
        )
    tile = 256
    return pl.pallas_call(
        functools.partial(up_kernel, offsets, depth),
        grid_spec=pltpu.PrefetchScalarGridSpec(
            num_scalar_prefetch=1,
            grid=(rows // tile,),
            in_specs=[
                pl.BlockSpec((tile, width_model), lambda r, s: (r, 0)),
                pl.BlockSpec((tile, 1), lambda r, s: (r, 0)),
            ]
            + specs,
            out_specs=pl.BlockSpec((tile, joint_width // 2), lambda r, s: (r, 0)),
        ),
        out_shape=jax.ShapeDtypeStruct((rows, joint_width // 2), jnp.bfloat16),
        compiler_params=pltpu.CompilerParams(vmem_limit_bytes=48 * 2**20),
        cost_estimate=pl.CostEstimate(
            flops=0,
            bytes_accessed=0,
            transcendentals=0,
        ),
    )(index, tokens, gate, *operands)


def down_kernel(h0_ref, h1_ref, w0_ref, w1_ref, out_ref):
    nt = (((1,), (1,)), ((), ()))
    out = lax.dot_general(h0_ref[...], w0_ref[0], nt, preferred_element_type=jnp.float32)
    out += lax.dot_general(h1_ref[...], w1_ref[0], nt, preferred_element_type=jnp.float32)
    out_ref[...] = out.astype(jnp.bfloat16)


def down(hidden, parts):
    rows, width = hidden[0].shape
    per = parts[0].shape[0]
    depth = parts[0].shape[1]
    tile = 256
    spec_h = pl.BlockSpec((tile, width), lambda r: (r, 0))

    def spec_w(expert):
        return pl.BlockSpec((1, depth, width), lambda r, at=expert % per: (at, 0, 0))

    return pl.pallas_call(
        down_kernel,
        grid=(rows // tile,),
        in_specs=[spec_h, spec_h, spec_w(0), spec_w(1)],
        out_specs=pl.BlockSpec((tile, depth), lambda r: (r, 0)),
        out_shape=jax.ShapeDtypeStruct((rows, depth), jnp.bfloat16),
        compiler_params=pltpu.CompilerParams(vmem_limit_bytes=48 * 2**20),
        cost_estimate=pl.CostEstimate(
            flops=0,
            bytes_accessed=0,
            transcendentals=0,
        ),
    )(hidden[0], hidden[1], parts[0], parts[1 // per])


def return_blocks(partial, rows):
    turns = lax.axis_size("ctx") // CORES
    count = turns * rows
    arrived = flip(partial[count:], "ctx", 1)
    both = partial[:count].astype(jnp.float32) + arrived.astype(jnp.float32)
    sent = both[rows:].astype(jnp.bfloat16)
    total = both[:rows]
    for d in range(1, turns):
        total += turn(sent[(d - 1) * rows : d * rows], turns - d).astype(jnp.float32)
    return total.astype(jnp.bfloat16), [sent]


def per_device(
    inputs,
    queries,
    kv_down,
    latent_gain,
    kv_up,
    out_proj,
    post_gain,
    expert_ids,
    gates,
    gate_up,
    down_proj,
):
    tokens = inputs[0]
    rows = tokens.shape[0]
    width_model = tokens.shape[1]
    ctx_size = lax.axis_size("ctx")
    rank = lax.axis_index("ctx")
    here = lax.axis_index("fsdp")
    turns = ctx_size // CORES
    local_experts = gate_up.shape[0]
    experts = local_experts * ctx_size

    up_pieces = first_step(gate_up)
    up_far = second_step(up_pieces)
    last_up = [p for o in sorted(up_far) for p in up_far[o]]
    down_pieces = first_step(after(down_proj, *last_up))
    down_pieces.update(second_step(down_pieces))

    row_iota = jnp.arange(rows, dtype=jnp.int32)
    positions = rank * rows + row_iota
    angles = angles_of(positions, ROPE)
    latent_width = latent_gain.shape[0]
    compressed = jnp.dot(tokens, kv_down, preferred_element_type=jnp.float32)
    latent = normalize(compressed[:, :latent_width], latent_gain)
    key_rope = rotate(compressed[:, latent_width:], angles)

    chosen = expert_ids[0][:, :, None] == jnp.arange(experts, dtype=jnp.int32)
    table = jnp.sum(jnp.where(chosen, gates[0][:, :, None], 0.0), axis=1)
    table_high = table.astype(jnp.bfloat16)
    table_low = (table - table_high.astype(jnp.float32)).astype(jnp.bfloat16)
    cache = jnp.concatenate(
        [latent.astype(jnp.bfloat16), key_rope.astype(jnp.bfloat16), table_high, table_low], axis=1
    )
    mine, other = gather_blocks(cache)
    every = jnp.concatenate([mine, other]).reshape(ctx_size * rows, cache.shape[1])
    key_width = latent_width + ROPE
    keys = every[:, :key_width]
    z = rank // CORES
    core = rank % CORES
    owners = jnp.concatenate(
        [
            jnp.stack([((z - d) % turns) * CORES + core for d in range(turns)]),
            jnp.stack([((z - d) % turns) * CORES + 1 - core for d in range(turns)]),
        ]
    )
    key_pos = (owners[:, None] * rows + row_iota[None, :]).reshape(-1)
    table_all = every[:, key_width:].astype(jnp.float32)
    table_all = table_all[:, :experts] + table_all[:, experts : 2 * experts]
    gate_columns = lax.dynamic_slice(
        table_all, (0, rank * local_experts), (ctx_size * rows, local_experts)
    )

    up_heads = kv_up.reshape(latent_width, HEADS, NOPE + VDIM)
    scale = (NOPE + ROPE) ** (-0.5)
    query_heads = queries[0].reshape(rows, HEADS, NOPE + ROPE)
    absorbed = jnp.einsum(
        "thn,lhn->htl",
        query_heads[:, :, :NOPE],
        up_heads[:, :, :NOPE],
        preferred_element_type=jnp.float32,
    )
    query_rope = rotate(query_heads[:, :, NOPE:].astype(jnp.float32), angles[:, None, :])
    query_rope = jnp.transpose(query_rope, (1, 0, 2))
    packed = (jnp.concatenate([absorbed, query_rope], axis=2) * scale).astype(jnp.bfloat16)
    packed = packed.reshape(HEADS * rows, key_width)
    row_pos = jnp.tile(positions, HEADS)
    scores = jnp.dot(packed, keys.T, preferred_element_type=jnp.float32)
    allowed = key_pos[None, :] <= row_pos[:, None]
    scores = jnp.where(allowed, scores, NEG_LARGE)
    peak = jnp.max(scores, axis=1, keepdims=True)
    expo = jnp.exp(scores - peak)
    total = jnp.sum(expo, axis=1)
    acc = jnp.dot(
        expo.astype(jnp.bfloat16), keys[:, :latent_width], preferred_element_type=jnp.float32
    )
    context = (acc / total[:, None]).astype(jnp.bfloat16).reshape(HEADS, rows, latent_width)
    heads = jnp.einsum(
        "htl,lhv->thv", context, up_heads[:, :, NOPE:], preferred_element_type=jnp.float32
    )
    heads = heads.astype(jnp.bfloat16).reshape(rows, HEADS * VDIM)
    attn = jnp.dot(heads, out_proj, preferred_element_type=jnp.float32)
    attn_out = attn.astype(jnp.bfloat16)
    routed_in = normalize(tokens.astype(jnp.float32) + attn, post_gain).astype(jnp.bfloat16)

    mine, other = gather_blocks(routed_in, up_pieces[1][0], up_pieces[2][0])
    up_pieces = {**up_pieces, **up_far}
    routed = jnp.concatenate([mine, other]).reshape(ctx_size * rows, width_model)
    index = jnp.reshape(here, (1,)).astype(jnp.int32)
    hidden = [
        up(index, routed, gate_columns[:, e : e + 1], e, up_pieces) for e in range(local_experts)
    ]
    depth = down_proj.shape[1]
    moe = jnp.zeros((rows, width_model), jnp.bfloat16)
    earlier = []
    for offset in sorted(down_pieces):
        held = after(tuple(hidden), *earlier) if earlier else hidden
        partial = down(held, down_pieces[offset])
        owned, earlier = return_blocks(partial, rows)
        moe = lax.dynamic_update_slice(moe, owned, (0, jnp.bitwise_xor(here, offset) * depth))
    return (attn_out[None], moe[None])


def solution(mesh):
    in_specs = (
        P("fsdp", "ctx", None),
        P("fsdp", "ctx", None),
        P(),
        P(),
        P(),
        P(),
        P(),
        P("fsdp", "ctx", None),
        P("fsdp", "ctx", None),
        P("ctx", "fsdp", None),
        P("ctx", "fsdp", None),
    )
    out_specs = (P("fsdp", "ctx", None), P("fsdp", "ctx", None))
    return jax.shard_map(
        per_device, mesh=mesh, in_specs=in_specs, out_specs=out_specs, check_vma=False
    )
```

```python
import functools
import math

import jax
import jax.numpy as jnp
from jax import lax
from jax.experimental import pallas as pl
from jax.experimental.pallas import tpu as pltpu
from jax.sharding import PartitionSpec as P

HEADS = 16
NOPE = 128
ROPE = 64
VDIM = 128
LANES = 128

EPSILON = 1e-06
NEG_LARGE = -1e30
CORES = 2
NT = (((1,), (1,)), ((), ()))
MEMORY = 56 * 2**20
WEIGHT = 20


def dot(left, right):
    return jnp.dot(left, right, preferred_element_type=jnp.float32)


def dot_nt(left, right):
    return lax.dot_general(left, right, NT, preferred_element_type=jnp.float32)


def free():
    return pl.CostEstimate(flops=0, bytes_accessed=0, transcendentals=0)


def normalize(values, gain):
    mean_sq = jnp.mean(values * values, axis=-1, keepdims=True)
    return values * lax.rsqrt(mean_sq + EPSILON) * gain


def swing_tables(positions):
    half = ROPE // 2
    lane = jnp.arange(LANES, dtype=jnp.int32)
    turn_of = (lane % half).astype(jnp.float32)
    freqs = jnp.exp(-(2.0 * turn_of / ROPE) * math.log(10000.0))
    angles = positions.astype(jnp.float32)[:, None] * freqs[None, :]
    cosine = jnp.where(lane < ROPE, jnp.cos(angles), 0.0)
    sine = jnp.where(lane < half, -jnp.sin(angles), jnp.where(lane < ROPE, jnp.sin(angles), 0.0))
    return cosine, sine


def swing(values, cosine, sine):
    half = ROPE // 2
    lane = lax.broadcasted_iota(jnp.int32, values.shape, 1)
    swapped = jnp.where(
        lane < half, pltpu.roll(values, LANES - half, 1), pltpu.roll(values, half, 1)
    )
    return values * cosine + swapped * sine


def flip(values, axis, mask):
    size = lax.axis_size(axis)
    return lax.ppermute(values, axis, [(i, i ^ mask) for i in range(size)])


def turn(values, step):
    size = lax.axis_size("ctx")
    return lax.ppermute(values, "ctx", [(i, (i + CORES * step) % size) for i in range(size)])


def after(value, *earlier):
    return lax.optimization_barrier((value, *earlier))[0]


def first_step(shard):
    return {0: [shard], 1: [flip(shard, "fsdp", 1)], 2: [flip(shard, "fsdp", 2)]}


def second_step(pieces):
    size = lax.axis_size("fsdp")
    half = pieces[0][0].shape[0] // 2
    if size == 4:
        low_half, high_half = pieces[1][0][:half], pieces[2][0][half:]
        low = flip(low_half, "fsdp", 2)
        high = flip(high_half, "fsdp", 1)
        return {3: [low, high]}, [low_half, high_half]
    more = {3: [flip(pieces[1][0], "fsdp", 2)]}
    held = {**pieces, **more}
    bit = 4
    while bit < size:
        new = {o | bit: [flip(p[0], "fsdp", bit)] for o, p in held.items()}
        more.update(new)
        held.update(new)
        bit *= 2
    return more, []


def compress_kernel(
    experts, token_ref, kv_ref, gain_ref, cos_ref, sin_ref, ids_ref, gates_ref, out_ref, pad_ref
):
    width = gain_ref.shape[1]
    compressed = dot_nt(token_ref[...], kv_ref[...])
    latent = normalize(compressed[:, :width], gain_ref[...].astype(jnp.float32))
    out_ref[:, :width] = latent.astype(jnp.bfloat16)
    pad_ref[...] = jnp.zeros_like(pad_ref)
    pad_ref[:, :ROPE] = compressed[:, width:]
    swung = swing(pad_ref[...], cos_ref[...], sin_ref[...])
    lane = lax.broadcasted_iota(jnp.int32, swung.shape, 1)
    ids = ids_ref[...]
    gates = gates_ref[...]
    table = jnp.zeros_like(swung)
    for k in range(ids.shape[1]):
        pick = ids[:, k : k + 1] + ROPE
        named = (pick == lane) | (pick + experts == lane)
        table += jnp.where(named, gates[:, k : k + 1], 0.0)
    high = table.astype(jnp.bfloat16).astype(jnp.float32)
    table = jnp.where(lane < ROPE + experts, high, table - high)
    out_ref[:, width:] = jnp.where(lane < ROPE, swung, table).astype(jnp.bfloat16)


def compress(tokens, kv_down, latent_gain, cosine, sine, ids, gates, experts):
    rows = tokens.shape[0]
    return pl.pallas_call(
        functools.partial(compress_kernel, experts),
        out_shape=jax.ShapeDtypeStruct((rows, latent_gain.shape[0] + LANES), jnp.bfloat16),
        scratch_shapes=[pltpu.VMEM((rows, LANES), jnp.float32)],
        compiler_params=pltpu.CompilerParams(vmem_limit_bytes=MEMORY),
        cost_estimate=free(),
    )(tokens, kv_down.T, latent_gain[None, :], cosine, sine, ids, gates)


def attend_kernel(
    pairs,
    blocks,
    query_ref,
    up_ref,
    key_pos_ref,
    row_pos_ref,
    cos_ref,
    sin_ref,
    out_proj_ref,
    token_ref,
    gain_ref,
    *refs,
):
    key_refs = refs[:blocks]
    attn_ref, routed_ref, acc_ref, packed_ref, bias_ref, keys_ref = refs[blocks:]
    rows = token_ref.shape[0]
    latent_width = up_ref.shape[0]
    head_width = NOPE + VDIM
    scale = (NOPE + ROPE) ** (-0.5)
    step = pl.program_id(0)

    @pl.when(step == 0)
    def _():
        acc_ref[...] = jnp.zeros_like(acc_ref)
        bias_ref[...] = jnp.where(key_pos_ref[...] <= row_pos_ref[...], 0.0, NEG_LARGE)
        for i, ref in enumerate(key_refs):
            keys_ref[i * rows : (i + 1) * rows, :] = ref[...]

    cosine, sine = cos_ref[...], sin_ref[...]
    lane = lax.broadcasted_iota(jnp.int32, (rows, LANES), 1)
    for pair in range(pairs):
        base = pair * 2 * (NOPE + ROPE)
        middle = query_ref[:, base + LANES : base + 2 * LANES].astype(jnp.float32)
        last = query_ref[:, base + 2 * LANES : base + 3 * LANES].astype(jnp.float32)
        middle_back, last_back = pltpu.roll(middle, ROPE, 1), pltpu.roll(last, ROPE, 1)
        plain = (
            query_ref[:, base : base + LANES],
            jnp.where(lane < ROPE, middle_back, last_back).astype(jnp.bfloat16),
        )
        turned = (middle, last_back)
        for h in range(2):
            at = (pair * 2 + h) * head_width
            here = slice((pair * 2 + h) * rows, (pair * 2 + h + 1) * rows)
            absorbed = dot_nt(plain[h], up_ref[:, at : at + NOPE])
            packed_ref[here, :latent_width] = (absorbed * scale).astype(jnp.bfloat16)
            swung = swing(turned[h], cosine, sine)
            packed_ref[here, latent_width:] = (swung * scale).astype(jnp.bfloat16)
        packed = packed_ref[pair * 2 * rows : (pair + 1) * 2 * rows, :]
        scores = dot_nt(packed, keys_ref[...])
        bias = bias_ref[...]
        scores = scores + jnp.concatenate([bias, bias], axis=0)
        expo = jnp.exp(scores - jnp.max(scores, axis=1, keepdims=True))
        total = jnp.sum(expo, axis=1, keepdims=True)
        context = dot(expo.astype(jnp.bfloat16), keys_ref[:, :latent_width])
        context = (context / total).astype(jnp.bfloat16)
        heads = []
        for h in range(2):
            at = (pair * 2 + h) * head_width + NOPE
            heads.append(dot(context[h * rows : (h + 1) * rows], up_ref[:, at : at + VDIM]))
        heads = jnp.concatenate(heads, axis=1).astype(jnp.bfloat16)
        acc_ref[...] += dot(heads, out_proj_ref[pair * 2 * VDIM : (pair + 1) * 2 * VDIM, :])

    @pl.when(step == pl.num_programs(0) - 1)
    def _():
        attn = acc_ref[...]
        attn_ref[...] = attn.astype(jnp.bfloat16)
        routed = normalize(
            token_ref[...].astype(jnp.float32) + attn, gain_ref[...].astype(jnp.float32)
        )
        routed_ref[...] = routed.astype(jnp.bfloat16)


def attend(queries, kv_up, keys, key_pos, row_pos, cosine, sine, out_proj, tokens, post_gain):
    rows, width_model = tokens.shape
    pairs = 2
    steps = HEADS // (2 * pairs)
    latent_width = kv_up.shape[0]
    key_width = keys[0].shape[1]
    count = key_pos.shape[1]

    def whole(*shape):
        return pl.BlockSpec(shape, lambda i: (0, 0))

    return pl.pallas_call(
        functools.partial(attend_kernel, pairs, len(keys)),
        grid=(steps,),
        in_specs=[
            pl.BlockSpec((rows, pairs * 2 * (NOPE + ROPE)), lambda i: (0, i)),
            pl.BlockSpec((latent_width, pairs * 2 * (NOPE + VDIM)), lambda i: (0, i)),
            whole(1, count),
            whole(rows, 1),
            whole(rows, LANES),
            whole(rows, LANES),
            pl.BlockSpec((pairs * 2 * VDIM, width_model), lambda i: (i, 0)),
            whole(rows, width_model),
            whole(1, width_model),
        ]
        + [whole(rows, key_width)] * len(keys),
        out_specs=[whole(rows, width_model)] * 2,
        out_shape=[jax.ShapeDtypeStruct((rows, width_model), jnp.bfloat16)] * 2,
        scratch_shapes=[
            pltpu.VMEM((rows, width_model), jnp.float32),
            pltpu.VMEM((pairs * 2 * rows, key_width), jnp.bfloat16),
            pltpu.VMEM((rows, count), jnp.float32),
            pltpu.VMEM((count, key_width), jnp.bfloat16),
        ],
        compiler_params=pltpu.CompilerParams(vmem_limit_bytes=MEMORY),
        cost_estimate=free(),
    )(
        queries,
        kv_up,
        key_pos,
        row_pos,
        cosine,
        sine,
        out_proj,
        tokens,
        post_gain[None, :],
        *keys,
    )


def up_kernel(offsets, depth, expert, experts, blocks, index_ref, *refs):
    x_refs, table_refs = refs[:blocks], refs[blocks : 2 * blocks]
    weights = refs[2 * blocks : -1]
    gate_weights, up_weights = weights[: len(offsets)], weights[len(offsets) :]
    out_ref = refs[-1]
    me = index_ref[0]
    named = index_ref[1] + expert + ROPE
    rows = x_refs[0].shape[0]
    for i in range(0, blocks, 2):
        gate_sum, up_sum = None, None
        for offset, gate_w, up_w in zip(offsets, gate_weights, up_weights):
            at = pl.ds(pl.multiple_of(jnp.bitwise_xor(me, offset) * depth, depth), depth)
            x = jnp.concatenate([x_refs[i][:, at], x_refs[i + 1][:, at]], axis=0)
            gate_term, up_term = dot(x, gate_w[0]), dot(x, up_w[0])
            gate_sum = gate_term if gate_sum is None else gate_sum + gate_term
            up_sum = up_term if up_sum is None else up_sum + up_term
        table = jnp.concatenate([table_refs[i][...], table_refs[i + 1][...]], axis=0)
        lane = lax.broadcasted_iota(jnp.int32, table.shape, 1)
        mine = (lane == named) | (lane == named + experts)
        gate = jnp.sum(jnp.where(mine, table.astype(jnp.float32), 0.0), axis=1, keepdims=True)
        hidden = gate_sum / (1.0 + jnp.exp(-gate_sum)) * up_sum * gate
        out_ref[i * rows : (i + 2) * rows, :] = hidden.astype(jnp.bfloat16)


def up(index, tokens, tables, expert, experts, pieces):
    rows, width_model = tokens[0].shape
    blocks = len(tokens)
    offsets = sorted(pieces)
    depth, joint_width = pieces[0][0].shape[1:]
    width = joint_width // 2
    tile = 256
    tiles = width // tile
    operands, gate_specs, up_specs = [], [], []
    for offset in offsets:
        parts = pieces[offset]
        per = parts[0].shape[0]
        operands.append(parts[expert // per])
        at = expert % per
        gate_specs.append(pl.BlockSpec((1, depth, tile), lambda j, s, at=at: (at, 0, j)))
        up_specs.append(pl.BlockSpec((1, depth, tile), lambda j, s, at=at: (at, 0, j + tiles)))
    last = tables[0].shape[1] // LANES - 1
    return pl.pallas_call(
        functools.partial(up_kernel, offsets, depth, expert, experts, blocks),
        grid_spec=pltpu.PrefetchScalarGridSpec(
            num_scalar_prefetch=1,
            grid=(tiles,),
            in_specs=[pl.BlockSpec((rows, width_model), lambda j, s: (0, 0))] * blocks
            + [pl.BlockSpec((rows, LANES), lambda j, s: (0, last))] * blocks
            + gate_specs
            + up_specs,
            out_specs=pl.BlockSpec((blocks * rows, tile), lambda j, s: (0, j)),
        ),
        out_shape=jax.ShapeDtypeStruct((blocks * rows, width), jnp.bfloat16),
        compiler_params=pltpu.CompilerParams(vmem_limit_bytes=MEMORY),
        cost_estimate=free(),
    )(index, *tokens, *tables, *operands, *operands)


def product(hidden_refs, weights, at, part):
    return dot_nt(hidden_refs[0][at, :], weights[2 * part][0]) + dot_nt(
        hidden_refs[1][at, :], weights[2 * part + 1][0]
    )


def down_kernel(blocks, parts, *refs):
    hidden, weights, out_ref = refs[:2], refs[2:-1], refs[-1]
    rows = hidden[0].shape[0] // blocks
    depth = out_ref.shape[1] // parts
    for i in range(1, blocks, 2):
        at = slice(i * rows, (i + 1) * rows)
        for part in range(parts):
            out = product(hidden, weights, at, part)
            out_ref[i // 2 * rows : (i // 2 + 1) * rows, part * depth : (part + 1) * depth] = (
                out.astype(jnp.bfloat16)
            )


def down_add_kernel(blocks, parts, *refs):
    hidden, weights, arrived_ref = refs[:2], refs[2 : 2 + 2 * parts], refs[2 + 2 * parts]
    own_ref, *out_refs = refs[3 + 2 * parts :]
    rows = hidden[0].shape[0] // blocks
    depth = own_ref.shape[1] // parts
    for i in range(0, blocks, 2):
        at = slice(i * rows, (i + 1) * rows)
        for part in range(parts):
            columns = slice(part * depth, (part + 1) * depth)
            out = product(hidden, weights, at, part)
            out += arrived_ref[i // 2 * rows : (i // 2 + 1) * rows, columns].astype(jnp.float32)
            if i == 0:
                own_ref[:, columns] = out
            else:
                out_refs[i // 2 - 1][:, columns] = out.astype(jnp.bfloat16)


def down_and_return(hidden, pieces, blocks):
    total_rows, width = hidden[0].shape
    rows = total_rows // blocks
    depth = pieces[0][0].shape[1]
    turns = blocks // CORES
    count = len(pieces)
    columns = count * depth

    def whole(*shape):
        return pl.BlockSpec(shape, lambda i: (0, 0))

    specs = [whole(total_rows, width)] * 2
    operands = list(hidden)
    for parts in pieces:
        per = parts[0].shape[0]
        for expert in range(2):
            specs.append(
                pl.BlockSpec((1, depth, width), lambda i, at=expert % per: (at, 0, 0))
            )
            operands.append(parts[expert // per])
    params = pltpu.CompilerParams(vmem_limit_bytes=MEMORY)
    cost = pl.CostEstimate(
        flops=WEIGHT * total_rows * width * columns, bytes_accessed=0, transcendentals=0
    )
    partial = pl.pallas_call(
        functools.partial(down_kernel, blocks, count),
        grid=(1,),
        in_specs=specs,
        out_specs=whole(turns * rows, columns),
        out_shape=jax.ShapeDtypeStruct((turns * rows, columns), jnp.bfloat16),
        compiler_params=params,
        cost_estimate=cost,
    )(*operands)
    arrived = flip(partial, "ctx", 1)
    own, *sent = pl.pallas_call(
        functools.partial(down_add_kernel, blocks, count),
        grid=(1,),
        in_specs=specs + [whole(turns * rows, columns)],
        out_specs=[whole(rows, columns)] * turns,
        out_shape=[jax.ShapeDtypeStruct((rows, columns), jnp.float32)]
        + [jax.ShapeDtypeStruct((rows, columns), jnp.bfloat16)] * (turns - 1),
        compiler_params=params,
        cost_estimate=cost,
    )(*operands, arrived)
    home = [turn(sent[d - 1], turns - d) for d in range(1, turns)]
    total = own
    for block in home:
        total += block.astype(jnp.float32)
    return total.astype(jnp.bfloat16), sent


def per_device(
    inputs,
    queries,
    kv_down,
    latent_gain,
    kv_up,
    out_proj,
    post_gain,
    expert_ids,
    gates,
    gate_up,
    down_proj,
):
    tokens = inputs[0]
    rows, width_model = tokens.shape
    ctx_size = lax.axis_size("ctx")
    rank = lax.axis_index("ctx")
    here = lax.axis_index("fsdp")
    turns = ctx_size // CORES
    local_experts = gate_up.shape[0]
    experts = local_experts * ctx_size

    up_pieces = first_step(gate_up)

    row_iota = jnp.arange(rows, dtype=jnp.int32)
    positions = rank * rows + row_iota
    cosine, sine = swing_tables(positions)
    cache = compress(
        tokens, kv_down, latent_gain, cosine, sine, expert_ids[0], gates[0], experts
    )
    mine = [cache] + [turn(cache, d) for d in range(1, turns)]
    other = flip(jnp.stack(mine), "ctx", 1)
    keys = [block for d in range(turns) for block in (mine[d], other[d])]
    z = rank // CORES
    core = rank % CORES
    owners = jnp.stack(
        [(z - d) % turns * CORES + side for d in range(turns) for side in (core, 1 - core)]
    )
    key_pos = (owners[:, None] * rows + row_iota[None, :]).reshape(1, -1)
    attn_out, routed = attend(
        queries[0],
        kv_up,
        keys,
        key_pos,
        positions[:, None],
        cosine,
        sine,
        out_proj,
        tokens,
        post_gain,
    )

    near = (1, turns - 1)
    mine = {0: routed, **{d: turn(routed, d) for d in near}}
    up_pieces = {o: [after(p[0], *[mine[d] for d in near])] for o, p in up_pieces.items()}
    up_far, up_halves = second_step(up_pieces)
    late = after(routed, up_pieces[1][0], up_pieces[2][0], *up_halves)
    mine.update({d: turn(late, d) for d in range(1, turns) if d not in near})
    gathered = [block for d in range(turns) for block in (mine[d], flip(mine[d], "ctx", 1))]
    last_up = [p for o in sorted(up_far) for p in up_far[o]]
    down_pieces = first_step(after(down_proj, *last_up, *gathered))
    down_far, down_halves = second_step(down_pieces)
    index = jnp.stack([here, rank * local_experts]).astype(jnp.int32)
    up_pieces = {**up_pieces, **up_far}
    down_pieces = {**down_pieces, **down_far}
    hidden = [
        up(index, gathered, keys, e, experts, up_pieces) for e in range(local_experts)
    ]
    depth = down_proj.shape[1]
    moe = jnp.zeros((rows, width_model), jnp.bfloat16)
    earlier = []
    for offsets in ((0,), (1, 2), tuple(sorted(down_far))):
        held = after(tuple(hidden), *earlier) if earlier else hidden
        pieces = [down_pieces[offset] for offset in offsets]
        owned, sent = down_and_return(held, pieces, ctx_size)
        earlier = [*sent, *down_halves] if 0 in offsets else sent
        for part, offset in enumerate(offsets):
            columns = owned[:, part * depth : (part + 1) * depth]
            start = jnp.bitwise_xor(here, offset) * depth
            moe = lax.dynamic_update_slice(moe, columns, (0, start))
    return (attn_out[None], moe[None])


def solution(mesh):
    in_specs = (
        P("fsdp", "ctx", None),
        P("fsdp", "ctx", None),
        P(),
        P(),
        P(),
        P(),
        P(),
        P("fsdp", "ctx", None),
        P("fsdp", "ctx", None),
        P("ctx", "fsdp", None),
        P("ctx", "fsdp", None),
    )
    out_specs = (P("fsdp", "ctx", None), P("fsdp", "ctx", None))
    return jax.shard_map(
        per_device, mesh=mesh, in_specs=in_specs, out_specs=out_specs, check_vma=False
    )
```

```python
import functools
import math

import jax
import jax.numpy as jnp
from jax import lax
from jax.experimental import pallas as pl
from jax.experimental.pallas import tpu as pltpu
from jax.sharding import PartitionSpec as P

HEADS = 16
NOPE = 128
ROPE = 64
VDIM = 128
LANES = 128

EPSILON = 1e-06
NEG_LARGE = -1e30
CORES = 2
NT = (((1,), (1,)), ((), ()))
MEMORY = 56 * 2**20
WEIGHT = 20
CHUNK = 512


def dot(left, right):
    return jnp.dot(left, right, preferred_element_type=jnp.float32)


def dot_nt(left, right):
    return lax.dot_general(left, right, NT, preferred_element_type=jnp.float32)


def free():
    return pl.CostEstimate(flops=0, bytes_accessed=0, transcendentals=0)


def normalize(values, gain):
    mean_sq = jnp.mean(values * values, axis=-1, keepdims=True)
    return values * lax.rsqrt(mean_sq + EPSILON) * gain


def swing_tables(positions):
    half = ROPE // 2
    lane = jnp.arange(LANES, dtype=jnp.int32)
    turn_of = (lane % half).astype(jnp.float32)
    freqs = jnp.exp(-(2.0 * turn_of / ROPE) * math.log(10000.0))
    angles = positions.astype(jnp.float32)[:, None] * freqs[None, :]
    cosine = jnp.where(lane < ROPE, jnp.cos(angles), 0.0)
    sine = jnp.where(lane < half, -jnp.sin(angles), jnp.where(lane < ROPE, jnp.sin(angles), 0.0))
    return cosine, sine


def swing(values, cosine, sine):
    half = ROPE // 2
    lane = lax.broadcasted_iota(jnp.int32, values.shape, 1)
    swapped = jnp.where(
        lane < half, pltpu.roll(values, LANES - half, 1), pltpu.roll(values, half, 1)
    )
    return values * cosine + swapped * sine


def flip(values, axis, mask):
    size = lax.axis_size(axis)
    return lax.ppermute(values, axis, [(i, i ^ mask) for i in range(size)])


def turn(values, step):
    size = lax.axis_size("ctx")
    return lax.ppermute(values, "ctx", [(i, (i + CORES * step) % size) for i in range(size)])


def after(value, *earlier):
    return lax.optimization_barrier((value, *earlier))[0]


def first_step(shard):
    return {0: [shard], 1: [flip(shard, "fsdp", 1)], 2: [flip(shard, "fsdp", 2)]}


def second_step(pieces):
    size = lax.axis_size("fsdp")
    half = pieces[0][0].shape[0] // 2
    if size == 4:
        low_half, high_half = pieces[1][0][:half], pieces[2][0][half:]
        low = flip(low_half, "fsdp", 2)
        high = flip(high_half, "fsdp", 1)
        return {3: [low, high]}, [low_half, high_half]
    more = {3: [flip(pieces[1][0], "fsdp", 2)]}
    held = {**pieces, **more}
    bit = 4
    while bit < size:
        new = {o | bit: [flip(p[0], "fsdp", bit)] for o, p in held.items()}
        more.update(new)
        held.update(new)
        bit *= 2
    return more, []


def compress_kernel(
    experts, token_ref, kv_ref, gain_ref, cos_ref, sin_ref, ids_ref, gates_ref, out_ref, pad_ref
):
    width = gain_ref.shape[1]
    compressed = dot_nt(token_ref[...], kv_ref[...])
    latent = normalize(compressed[:, :width], gain_ref[...].astype(jnp.float32))
    out_ref[:, :width] = latent.astype(jnp.bfloat16)
    pad_ref[...] = jnp.zeros_like(pad_ref)
    pad_ref[:, :ROPE] = compressed[:, width:]
    swung = swing(pad_ref[...], cos_ref[...], sin_ref[...])
    lane = lax.broadcasted_iota(jnp.int32, swung.shape, 1)
    ids = ids_ref[...]
    gates = gates_ref[...]
    table = jnp.zeros_like(swung)
    for k in range(ids.shape[1]):
        pick = ids[:, k : k + 1] + ROPE
        named = (pick == lane) | (pick + experts == lane)
        table += jnp.where(named, gates[:, k : k + 1], 0.0)
    high = table.astype(jnp.bfloat16).astype(jnp.float32)
    table = jnp.where(lane < ROPE + experts, high, table - high)
    out_ref[:, width:] = jnp.where(lane < ROPE, swung, table).astype(jnp.bfloat16)


def compress(tokens, kv_down, latent_gain, cosine, sine, ids, gates, experts):
    rows = tokens.shape[0]
    return pl.pallas_call(
        functools.partial(compress_kernel, experts),
        out_shape=jax.ShapeDtypeStruct((rows, latent_gain.shape[0] + LANES), jnp.bfloat16),
        scratch_shapes=[pltpu.VMEM((rows, LANES), jnp.float32)],
        compiler_params=pltpu.CompilerParams(vmem_limit_bytes=MEMORY),
        cost_estimate=free(),
    )(tokens, kv_down.T, latent_gain[None, :], cosine, sine, ids, gates)


def attend_kernel(
    pairs,
    blocks,
    query_ref,
    up_ref,
    key_pos_ref,
    row_pos_ref,
    cos_ref,
    sin_ref,
    out_proj_ref,
    token_ref,
    gain_ref,
    *refs,
):
    key_refs = refs[:blocks]
    attn_ref, routed_ref, acc_ref, packed_ref, bias_ref, keys_ref, turned_ref = refs[blocks:]
    rows = token_ref.shape[0]
    latent_width = up_ref.shape[0]
    head_width = NOPE + VDIM
    scale = (NOPE + ROPE) ** (-0.5)
    step = pl.program_id(0)

    @pl.when(step == 0)
    def _():
        acc_ref[...] = jnp.zeros_like(acc_ref)
        bias_ref[...] = jnp.where(key_pos_ref[...] <= row_pos_ref[...], 0.0, NEG_LARGE)
        for i, ref in enumerate(key_refs):
            keys_ref[i * rows : (i + 1) * rows, :] = ref[...]
            turned_ref[:, i * rows : (i + 1) * rows] = ref[...].T

    cosine, sine = cos_ref[...], sin_ref[...]
    lane = lax.broadcasted_iota(jnp.int32, (rows, LANES), 1)
    for pair in range(pairs):
        base = pair * 2 * (NOPE + ROPE)
        middle = query_ref[:, base + LANES : base + 2 * LANES].astype(jnp.float32)
        last = query_ref[:, base + 2 * LANES : base + 3 * LANES].astype(jnp.float32)
        middle_back, last_back = pltpu.roll(middle, ROPE, 1), pltpu.roll(last, ROPE, 1)
        plain = (
            query_ref[:, base : base + LANES],
            jnp.where(lane < ROPE, middle_back, last_back).astype(jnp.bfloat16),
        )
        turned = (middle, last_back)
        for h in range(2):
            at = (pair * 2 + h) * head_width
            here = slice((pair * 2 + h) * rows, (pair * 2 + h + 1) * rows)
            absorbed = dot_nt(plain[h], up_ref[:, at : at + NOPE])
            packed_ref[here, :latent_width] = (absorbed * scale).astype(jnp.bfloat16)
            swung = swing(turned[h], cosine, sine)
            packed_ref[here, latent_width:] = (swung * scale).astype(jnp.bfloat16)
        packed = packed_ref[pair * 2 * rows : (pair + 1) * 2 * rows, :]
        scores = dot(packed, turned_ref[...])
        bias = bias_ref[...]
        scores = scores + jnp.concatenate([bias, bias], axis=0)
        expo = jnp.exp(scores - jnp.max(scores, axis=1, keepdims=True))
        total = jnp.sum(expo, axis=1, keepdims=True)
        context = dot(expo.astype(jnp.bfloat16), keys_ref[:, :latent_width])
        context = (context / total).astype(jnp.bfloat16)
        heads = []
        for h in range(2):
            at = (pair * 2 + h) * head_width + NOPE
            heads.append(dot(context[h * rows : (h + 1) * rows], up_ref[:, at : at + VDIM]))
        heads = jnp.concatenate(heads, axis=1).astype(jnp.bfloat16)
        acc_ref[...] += dot(heads, out_proj_ref[pair * 2 * VDIM : (pair + 1) * 2 * VDIM, :])

    @pl.when(step == pl.num_programs(0) - 1)
    def _():
        attn = acc_ref[...]
        attn_ref[...] = attn.astype(jnp.bfloat16)
        routed = normalize(
            token_ref[...].astype(jnp.float32) + attn, gain_ref[...].astype(jnp.float32)
        )
        routed_ref[...] = routed.astype(jnp.bfloat16)


def attend(queries, kv_up, keys, key_pos, row_pos, cosine, sine, out_proj, tokens, post_gain):
    rows, width_model = tokens.shape
    pairs = 2
    steps = HEADS // (2 * pairs)
    latent_width = kv_up.shape[0]
    key_width = keys[0].shape[1]
    count = key_pos.shape[1]

    def whole(*shape):
        return pl.BlockSpec(shape, lambda i: (0, 0))

    return pl.pallas_call(
        functools.partial(attend_kernel, pairs, len(keys)),
        grid=(steps,),
        in_specs=[
            pl.BlockSpec((rows, pairs * 2 * (NOPE + ROPE)), lambda i: (0, i)),
            pl.BlockSpec((latent_width, pairs * 2 * (NOPE + VDIM)), lambda i: (0, i)),
            whole(1, count),
            whole(rows, 1),
            whole(rows, LANES),
            whole(rows, LANES),
            pl.BlockSpec((pairs * 2 * VDIM, width_model), lambda i: (i, 0)),
            whole(rows, width_model),
            whole(1, width_model),
        ]
        + [whole(rows, key_width)] * len(keys),
        out_specs=[whole(rows, width_model)] * 2,
        out_shape=[jax.ShapeDtypeStruct((rows, width_model), jnp.bfloat16)] * 2,
        scratch_shapes=[
            pltpu.VMEM((rows, width_model), jnp.float32),
            pltpu.VMEM((pairs * 2 * rows, key_width), jnp.bfloat16),
            pltpu.VMEM((rows, count), jnp.float32),
            pltpu.VMEM((count, key_width), jnp.bfloat16),
            pltpu.VMEM((key_width, count), jnp.bfloat16),
        ],
        compiler_params=pltpu.CompilerParams(vmem_limit_bytes=MEMORY),
        cost_estimate=free(),
    )(
        queries,
        kv_up,
        key_pos,
        row_pos,
        cosine,
        sine,
        out_proj,
        tokens,
        post_gain[None, :],
        *keys,
    )


def up_kernel(layout, depth, experts, blocks, index_ref, *refs):
    x_refs, table_refs = refs[:blocks], refs[blocks : 2 * blocks]
    weights = refs[2 * blocks : -4]
    out_ref, x_ref, factor_ref, w_ref = refs[-4:]
    expert = pl.program_id(0)
    me = index_ref[0]
    named = index_ref[1] + expert + ROPE
    rows = x_refs[0].shape[0]
    tile = out_ref.shape[1]

    @pl.when((expert == 0) & (pl.program_id(1) == 0))
    def _():
        for i in range(blocks):
            place = (i % CORES) * (blocks // CORES) + i // CORES
            here = slice(place * rows, (place + 1) * rows)
            for part, (offset, _, _) in enumerate(layout):
                at = pl.ds(pl.multiple_of(jnp.bitwise_xor(me, offset) * depth, depth), depth)
                x_ref[here, part * depth : (part + 1) * depth] = x_refs[i][:, at]

    @pl.when(pl.program_id(1) == 0)
    def _():
        for i in range(blocks):
            place = (i % CORES) * (blocks // CORES) + i // CORES
            here = slice(place * rows, (place + 1) * rows)
            table = table_refs[i][...].astype(jnp.float32)
            lane = lax.broadcasted_iota(jnp.int32, table.shape, 1)
            mine = (lane == named) | (lane == named + experts)
            factor_ref[here, :] = jnp.sum(jnp.where(mine, table, 0.0), axis=1, keepdims=True)

    for part, (_, first, per) in enumerate(layout):
        here = slice(part * depth, (part + 1) * depth)

        def fill(at, here=here):
            w_ref[here, :tile] = weights[2 * at][0]
            w_ref[here, tile:] = weights[2 * at + 1][0]

        if per > 1:
            fill(first)
        else:
            pl.when(expert == 0)(functools.partial(fill, first))
            pl.when(expert == 1)(functools.partial(fill, first + 1))
    step = min(CHUNK, blocks * rows)
    for start in range(0, blocks * rows, step):
        here = slice(start, start + step)
        joint = dot(x_ref[here, :], w_ref[...])
        gate_sum, up_sum = joint[:, :tile], joint[:, tile:]
        hidden = gate_sum / (1.0 + jnp.exp(-gate_sum)) * up_sum * factor_ref[here, :]
        out_ref[here, :] = hidden.astype(jnp.bfloat16)


def up(index, tokens, tables, experts, pieces):
    rows, width_model = tokens[0].shape
    blocks = len(tokens)
    depth, joint_width = pieces[0][0].shape[1:]
    width = joint_width // 2
    tile = 256
    tiles = width // tile
    layout, operands, specs = [], [], []
    for offset in sorted(pieces):
        parts = pieces[offset]
        per = parts[0].shape[0]
        layout.append((offset, len(operands) // 2, per))
        for number, part in enumerate(parts):
            for side in range(2):

                def place(e, j, s, per=per, number=number, side=side):
                    if per > 1:
                        return e, 0, j + side * tiles
                    still = tiles - 1 if number == 0 else 0
                    return 0, 0, jnp.where(e == number, j, still) + side * tiles

                operands.append(part)
                specs.append(pl.BlockSpec((1, depth, tile), place))
    last = tables[0].shape[1] // LANES - 1
    return pl.pallas_call(
        functools.partial(up_kernel, layout, depth, experts, blocks),
        grid_spec=pltpu.PrefetchScalarGridSpec(
            num_scalar_prefetch=1,
            grid=(2, tiles),
            in_specs=[pl.BlockSpec((rows, width_model), lambda e, j, s: (0, 0))] * blocks
            + [pl.BlockSpec((rows, LANES), lambda e, j, s: (0, last))] * blocks
            + specs,
            out_specs=pl.BlockSpec((blocks * rows, tile), lambda e, j, s: (0, e * tiles + j)),
            scratch_shapes=[
                pltpu.VMEM((blocks * rows, width_model), jnp.bfloat16),
                pltpu.VMEM((blocks * rows, 1), jnp.float32),
                pltpu.VMEM((width_model, 2 * tile), jnp.bfloat16),
            ],
        ),
        out_shape=jax.ShapeDtypeStruct((blocks * rows, 2 * width), jnp.bfloat16),
        compiler_params=pltpu.CompilerParams(vmem_limit_bytes=MEMORY),
        cost_estimate=free(),
    )(index, *tokens, *tables, *operands)


def product(hidden, weights, part):
    first, second = weights[2 * part], weights[2 * part + 1]
    width = first.shape[2]
    return dot_nt(hidden[:, :width], first[0]) + dot_nt(hidden[:, width:], second[0])


def down_kernel(parts, *refs):
    hidden, weights, out_ref = refs[0], refs[1:-1], refs[-1]
    depth = out_ref.shape[1] // parts
    for part in range(parts):
        columns = slice(part * depth, (part + 1) * depth)
        out_ref[:, columns] = product(hidden, weights, part).astype(jnp.bfloat16)


def down_add_kernel(parts, *refs):
    hidden, weights, arrived_ref = refs[0], refs[1 : 1 + 2 * parts], refs[1 + 2 * parts]
    own_ref, *out_refs = refs[2 + 2 * parts :]
    rows, columns = own_ref.shape
    depth = columns // parts
    for part in range(parts):
        columns = slice(part * depth, (part + 1) * depth)
        out = product(hidden, weights, part) + arrived_ref[:, columns].astype(jnp.float32)
        own_ref[:, columns] = out[:rows]
        for i, out_ref in enumerate(out_refs):
            out_ref[:, columns] = out[(i + 1) * rows : (i + 2) * rows].astype(jnp.bfloat16)


def whole(*shape):
    return pl.BlockSpec(shape, lambda *i: (0,) * len(shape))


def down_operands(hidden, pieces, side):
    total_rows = hidden.shape[0]
    depth, width = pieces[0][0].shape[1:]
    specs = [pl.BlockSpec((total_rows // CORES, hidden.shape[1]), lambda i: (side, 0))]
    operands = [hidden]
    for parts in pieces:
        per = parts[0].shape[0]
        for expert in range(2):
            specs.append(
                pl.BlockSpec((1, depth, width), lambda i, at=expert % per: (at, 0, 0))
            )
            operands.append(parts[expert // per])
    cost = pl.CostEstimate(
        flops=WEIGHT * total_rows * width * depth * len(pieces),
        bytes_accessed=0,
        transcendentals=0,
    )
    params = pltpu.CompilerParams(vmem_limit_bytes=MEMORY)
    return specs, operands, dict(grid=(1,), compiler_params=params, cost_estimate=cost)


def down_first(hidden, pieces, blocks):
    specs, operands, options = down_operands(hidden, pieces, 1)
    shape = (hidden.shape[0] // CORES, len(pieces) * pieces[0][0].shape[1])
    return pl.pallas_call(
        functools.partial(down_kernel, len(pieces)),
        in_specs=specs,
        out_specs=whole(*shape),
        out_shape=jax.ShapeDtypeStruct(shape, jnp.bfloat16),
        **options,
    )(*operands)


def down_second(hidden, pieces, blocks, arrived):
    specs, operands, options = down_operands(hidden, pieces, 0)
    rows, columns = hidden.shape[0] // blocks, arrived.shape[1]
    turns = blocks // CORES
    return pl.pallas_call(
        functools.partial(down_add_kernel, len(pieces)),
        in_specs=specs + [whole(*arrived.shape)],
        out_specs=[whole(rows, columns)] * turns,
        out_shape=[jax.ShapeDtypeStruct((rows, columns), jnp.float32)]
        + [jax.ShapeDtypeStruct((rows, columns), jnp.bfloat16)] * (turns - 1),
        **options,
    )(*operands, arrived)


def down_and_return(hidden, pieces, blocks):
    turns = blocks // CORES
    arrived = flip(down_first(hidden, pieces, blocks), "ctx", 1)
    own, *sent = down_second(hidden, pieces, blocks, arrived)
    home = [turn(sent[d - 1], turns - d) for d in range(1, turns)]
    total = own
    for block in home:
        total += block.astype(jnp.float32)
    return total.astype(jnp.bfloat16), sent


def per_device(
    inputs,
    queries,
    kv_down,
    latent_gain,
    kv_up,
    out_proj,
    post_gain,
    expert_ids,
    gates,
    gate_up,
    down_proj,
):
    tokens = inputs[0]
    rows, width_model = tokens.shape
    ctx_size = lax.axis_size("ctx")
    rank = lax.axis_index("ctx")
    here = lax.axis_index("fsdp")
    turns = ctx_size // CORES
    local_experts = gate_up.shape[0]
    experts = local_experts * ctx_size

    up_pieces = first_step(gate_up)

    row_iota = jnp.arange(rows, dtype=jnp.int32)
    positions = rank * rows + row_iota
    cosine, sine = swing_tables(positions)
    cache = compress(
        tokens, kv_down, latent_gain, cosine, sine, expert_ids[0], gates[0], experts
    )
    mine = [cache] + [turn(cache, d) for d in range(1, turns)]
    keys = [block for cached in mine for block in (cached, flip(cached, "ctx", 1))]
    z = rank // CORES
    core = rank % CORES
    owners = jnp.stack(
        [(z - d) % turns * CORES + side for d in range(turns) for side in (core, 1 - core)]
    )
    key_pos = (owners[:, None] * rows + row_iota[None, :]).reshape(1, -1)
    attn_out, routed = attend(
        queries[0],
        kv_up,
        keys,
        key_pos,
        positions[:, None],
        cosine,
        sine,
        out_proj,
        tokens,
        post_gain,
    )

    near = (1, turns - 1)
    mine = {0: routed, **{d: turn(routed, d) for d in near}}
    up_pieces = {o: [after(p[0], mine[1])] for o, p in up_pieces.items()}
    up_far, up_halves = second_step(up_pieces)
    late = after(routed, up_pieces[1][0], up_pieces[2][0], *up_halves)
    mine.update({d: turn(late, d) for d in range(1, turns) if d not in near})
    gathered = [block for d in range(turns) for block in (mine[d], flip(mine[d], "ctx", 1))]
    last_up = [p for o in sorted(up_far) for p in up_far[o]]
    down_pieces = first_step(after(down_proj, *last_up, *gathered))
    down_far, down_halves = second_step(down_pieces)
    index = jnp.stack([here, rank * local_experts]).astype(jnp.int32)
    up_pieces = {**up_pieces, **up_far}
    down_pieces = {**down_pieces, **down_far}
    hidden = up(index, gathered, keys, experts, up_pieces)
    depth = down_proj.shape[1]
    moe = jnp.zeros((rows, width_model), jnp.bfloat16)
    earlier = []
    for offsets in ((0,), (1, 2), tuple(sorted(down_far))):
        held = after(hidden, *earlier) if earlier else hidden
        pieces = [down_pieces[offset] for offset in offsets]
        owned, sent = down_and_return(held, pieces, ctx_size)
        earlier = [*sent, *down_halves] if 0 in offsets else sent
        for part, offset in enumerate(offsets):
            columns = owned[:, part * depth : (part + 1) * depth]
            start = jnp.bitwise_xor(here, offset) * depth
            moe = lax.dynamic_update_slice(moe, columns, (0, start))
    return (attn_out[None], moe[None])


def solution(mesh):
    in_specs = (
        P("fsdp", "ctx", None),
        P("fsdp", "ctx", None),
        P(),
        P(),
        P(),
        P(),
        P(),
        P("fsdp", "ctx", None),
        P("fsdp", "ctx", None),
        P("ctx", "fsdp", None),
        P("ctx", "fsdp", None),
    )
    out_specs = (P("fsdp", "ctx", None), P("fsdp", "ctx", None))
    return jax.shard_map(
        per_device, mesh=mesh, in_specs=in_specs, out_specs=out_specs, check_vma=False
    )
```

```python
import functools
import math

import jax
import jax.numpy as jnp
from jax import lax
from jax.experimental import pallas as pl
from jax.experimental.pallas import tpu as pltpu
from jax.sharding import PartitionSpec as P

HEADS = 16
NOPE = 128
ROPE = 64
VDIM = 128
LANES = 128

EPSILON = 1e-06
NEG_LARGE = -1e30
CORES = 2
NT = (((1,), (1,)), ((), ()))
MEMORY = 56 * 2**20
CHUNK = 512


def dot(left, right):
    return jnp.dot(left, right, preferred_element_type=jnp.float32)


def dot_nt(left, right):
    return lax.dot_general(left, right, NT, preferred_element_type=jnp.float32)


def free():
    return pl.CostEstimate(flops=0, bytes_accessed=0, transcendentals=0)


def normalize(values, gain):
    mean_sq = jnp.mean(values * values, axis=-1, keepdims=True)
    return values * lax.rsqrt(mean_sq + EPSILON) * gain


def swing_tables(positions):
    half = ROPE // 2
    lane = jnp.arange(LANES, dtype=jnp.int32)
    turn_of = (lane % half).astype(jnp.float32)
    freqs = jnp.exp(-(2.0 * turn_of / ROPE) * math.log(10000.0))
    angles = positions.astype(jnp.float32)[:, None] * freqs[None, :]
    cosine = jnp.where(lane < ROPE, jnp.cos(angles), 0.0)
    sine = jnp.where(lane < half, -jnp.sin(angles), jnp.where(lane < ROPE, jnp.sin(angles), 0.0))
    return cosine, sine


def swing(values, cosine, sine):
    half = ROPE // 2
    lane = lax.broadcasted_iota(jnp.int32, values.shape, 1)
    swapped = jnp.where(
        lane < half, pltpu.roll(values, LANES - half, 1), pltpu.roll(values, half, 1)
    )
    return values * cosine + swapped * sine


def flip(values, axis, mask):
    size = lax.axis_size(axis)
    return lax.ppermute(values, axis, [(i, i ^ mask) for i in range(size)])


def turn(values, step):
    size = lax.axis_size("ctx")
    return lax.ppermute(values, "ctx", [(i, (i + CORES * step) % size) for i in range(size)])


def after(value, *earlier):
    return lax.optimization_barrier((value, *earlier))[0]


def first_step(shard):
    return {0: [shard], 1: [flip(shard, "fsdp", 1)], 2: [flip(shard, "fsdp", 2)]}


def second_step(pieces):
    size = lax.axis_size("fsdp")
    half = pieces[0][0].shape[0] // 2
    if size == 4:
        low_half, high_half = pieces[1][0][:half], pieces[2][0][half:]
        low = flip(low_half, "fsdp", 2)
        high = flip(high_half, "fsdp", 1)
        return {3: [low, high]}, [low_half, high_half]
    more = {3: [flip(pieces[1][0], "fsdp", 2)]}
    held = {**pieces, **more}
    bit = 4
    while bit < size:
        new = {o | bit: [flip(p[0], "fsdp", bit)] for o, p in held.items()}
        more.update(new)
        held.update(new)
        bit *= 2
    return more, []


def compress_kernel(
    experts, token_ref, kv_ref, gain_ref, cos_ref, sin_ref, ids_ref, gates_ref, out_ref, pad_ref
):
    width = gain_ref.shape[1]
    compressed = dot_nt(token_ref[...], kv_ref[...])
    latent = normalize(compressed[:, :width], gain_ref[...].astype(jnp.float32))
    out_ref[:, :width] = latent.astype(jnp.bfloat16)
    pad_ref[...] = jnp.zeros_like(pad_ref)
    pad_ref[:, :ROPE] = compressed[:, width:]
    swung = swing(pad_ref[...], cos_ref[...], sin_ref[...])
    lane = lax.broadcasted_iota(jnp.int32, swung.shape, 1)
    line = lax.broadcasted_iota(jnp.int32, swung.shape[::-1], 0)
    ids = ids_ref[...] + ROPE
    gates = gates_ref[...]
    table = jnp.zeros(line.shape, jnp.float32)
    for k in range(ids.shape[0]):
        pick = ids[k : k + 1, :]
        named = (pick == line) | (pick + experts == line)
        table += jnp.where(named, gates[k : k + 1, :], 0.0)
    table = table.T
    high = table.astype(jnp.bfloat16).astype(jnp.float32)
    table = jnp.where(lane < ROPE + experts, high, table - high)
    out_ref[:, width:] = jnp.where(lane < ROPE, swung, table).astype(jnp.bfloat16)


def compress(tokens, kv_down, latent_gain, cosine, sine, ids, gates, experts):
    rows = tokens.shape[0]
    return pl.pallas_call(
        functools.partial(compress_kernel, experts),
        out_shape=jax.ShapeDtypeStruct((rows, latent_gain.shape[0] + LANES), jnp.bfloat16),
        scratch_shapes=[pltpu.VMEM((rows, LANES), jnp.float32)],
        compiler_params=pltpu.CompilerParams(vmem_limit_bytes=MEMORY),
        cost_estimate=free(),
    )(tokens, kv_down.T, latent_gain[None, :], cosine, sine, ids, gates)


def attend_kernel(
    pairs,
    blocks,
    query_ref,
    up_ref,
    key_pos_ref,
    row_pos_ref,
    cos_ref,
    sin_ref,
    out_proj_ref,
    token_ref,
    gain_ref,
    *refs,
):
    key_refs = refs[:blocks]
    attn_ref, routed_ref, acc_ref, packed_ref, bias_ref, keys_ref, turned_ref = refs[blocks:]
    rows = token_ref.shape[0]
    latent_width = up_ref.shape[0]
    head_width = NOPE + VDIM
    scale = (NOPE + ROPE) ** (-0.5)
    step = pl.program_id(0)

    @pl.when(step == 0)
    def _():
        acc_ref[...] = jnp.zeros_like(acc_ref)
        bias_ref[...] = jnp.where(key_pos_ref[...] <= row_pos_ref[...], 0.0, NEG_LARGE)
        for i, ref in enumerate(key_refs):
            keys_ref[i * rows : (i + 1) * rows, :] = ref[...]
            turned_ref[:, i * rows : (i + 1) * rows] = ref[...].T

    cosine, sine = cos_ref[...], sin_ref[...]
    lane = lax.broadcasted_iota(jnp.int32, (rows, LANES), 1)
    for pair in range(pairs):
        base = pair * 2 * (NOPE + ROPE)
        middle = query_ref[:, base + LANES : base + 2 * LANES].astype(jnp.float32)
        last = query_ref[:, base + 2 * LANES : base + 3 * LANES].astype(jnp.float32)
        middle_back, last_back = pltpu.roll(middle, ROPE, 1), pltpu.roll(last, ROPE, 1)
        plain = (
            query_ref[:, base : base + LANES],
            jnp.where(lane < ROPE, middle_back, last_back).astype(jnp.bfloat16),
        )
        turned = (middle, last_back)
        for h in range(2):
            at = (pair * 2 + h) * head_width
            here = slice((pair * 2 + h) * rows, (pair * 2 + h + 1) * rows)
            absorbed = dot_nt(plain[h], up_ref[:, at : at + NOPE])
            packed_ref[here, :latent_width] = (absorbed * scale).astype(jnp.bfloat16)
            swung = swing(turned[h], cosine, sine)
            packed_ref[here, latent_width:] = (swung * scale).astype(jnp.bfloat16)
        packed = packed_ref[pair * 2 * rows : (pair + 1) * 2 * rows, :]
        scores = dot(packed, turned_ref[...])
        bias = bias_ref[...]
        scores = scores + jnp.concatenate([bias, bias], axis=0)
        expo = jnp.exp(scores - jnp.max(scores, axis=1, keepdims=True))
        total = jnp.sum(expo, axis=1, keepdims=True)
        context = dot(expo.astype(jnp.bfloat16), keys_ref[:, :latent_width])
        context = (context / total).astype(jnp.bfloat16)
        heads = []
        for h in range(2):
            at = (pair * 2 + h) * head_width + NOPE
            heads.append(dot(context[h * rows : (h + 1) * rows], up_ref[:, at : at + VDIM]))
        heads = jnp.concatenate(heads, axis=1).astype(jnp.bfloat16)
        acc_ref[...] += dot(heads, out_proj_ref[pair * 2 * VDIM : (pair + 1) * 2 * VDIM, :])

    @pl.when(step == pl.num_programs(0) - 1)
    def _():
        attn = acc_ref[...]
        attn_ref[...] = attn.astype(jnp.bfloat16)
        routed = normalize(
            token_ref[...].astype(jnp.float32) + attn, gain_ref[...].astype(jnp.float32)
        )
        routed_ref[...] = routed.astype(jnp.bfloat16)


def attend(queries, kv_up, keys, key_pos, row_pos, cosine, sine, out_proj, tokens, post_gain):
    rows, width_model = tokens.shape
    pairs = 2
    steps = HEADS // (2 * pairs)
    latent_width = kv_up.shape[0]
    key_width = keys[0].shape[1]
    count = key_pos.shape[1]

    def whole(*shape):
        return pl.BlockSpec(shape, lambda i: (0, 0))

    return pl.pallas_call(
        functools.partial(attend_kernel, pairs, len(keys)),
        grid=(steps,),
        in_specs=[
            pl.BlockSpec((rows, pairs * 2 * (NOPE + ROPE)), lambda i: (0, i)),
            pl.BlockSpec((latent_width, pairs * 2 * (NOPE + VDIM)), lambda i: (0, i)),
            whole(1, count),
            whole(rows, 1),
            whole(rows, LANES),
            whole(rows, LANES),
            pl.BlockSpec((pairs * 2 * VDIM, width_model), lambda i: (i, 0)),
            whole(rows, width_model),
            whole(1, width_model),
        ]
        + [whole(rows, key_width)] * len(keys),
        out_specs=[whole(rows, width_model)] * 2,
        out_shape=[jax.ShapeDtypeStruct((rows, width_model), jnp.bfloat16)] * 2,
        scratch_shapes=[
            pltpu.VMEM((rows, width_model), jnp.float32),
            pltpu.VMEM((pairs * 2 * rows, key_width), jnp.bfloat16),
            pltpu.VMEM((rows, count), jnp.float32),
            pltpu.VMEM((count, key_width), jnp.bfloat16),
            pltpu.VMEM((key_width, count), jnp.bfloat16),
        ],
        compiler_params=pltpu.CompilerParams(vmem_limit_bytes=MEMORY),
        cost_estimate=free(),
    )(
        queries,
        kv_up,
        key_pos,
        row_pos,
        cosine,
        sine,
        out_proj,
        tokens,
        post_gain,
        *keys,
    )


def up_kernel(layout, depth, experts, blocks, index_ref, *refs):
    x_refs, table_refs = refs[:blocks], refs[blocks : 2 * blocks]
    weights = refs[2 * blocks : -4]
    out_ref, x_ref, factor_ref, w_ref = refs[-4:]
    expert = pl.program_id(0)
    me = index_ref[0]
    named = index_ref[1] + expert + ROPE
    rows = x_refs[0].shape[0]
    tile = out_ref.shape[1]

    @pl.when((expert == 0) & (pl.program_id(1) == 0))
    def _():
        for i in range(blocks):
            place = (i % CORES) * (blocks // CORES) + i // CORES
            here = slice(place * rows, (place + 1) * rows)
            for part, (offset, _, _) in enumerate(layout):
                at = pl.ds(pl.multiple_of(jnp.bitwise_xor(me, offset) * depth, depth), depth)
                x_ref[here, part * depth : (part + 1) * depth] = x_refs[i][:, at]

    @pl.when(pl.program_id(1) == 0)
    def _():
        for i in range(blocks):
            place = (i % CORES) * (blocks // CORES) + i // CORES
            here = slice(place * rows, (place + 1) * rows)
            table = table_refs[i][...].astype(jnp.float32)
            lane = lax.broadcasted_iota(jnp.int32, table.shape, 1)
            mine = (lane == named) | (lane == named + experts)
            factor_ref[here, :] = jnp.sum(jnp.where(mine, table, 0.0), axis=1, keepdims=True)

    for part, (_, first, per) in enumerate(layout):
        here = slice(part * depth, (part + 1) * depth)

        def fill(at, here=here):
            w_ref[here, :tile] = weights[2 * at][0]
            w_ref[here, tile:] = weights[2 * at + 1][0]

        if per > 1:
            fill(first)
        else:
            pl.when(expert == 0)(functools.partial(fill, first))
            pl.when(expert == 1)(functools.partial(fill, first + 1))
    step = min(CHUNK, blocks * rows)
    for start in range(0, blocks * rows, step):
        here = slice(start, start + step)
        joint = dot(x_ref[here, :], w_ref[...])
        gate_sum, up_sum = joint[:, :tile], joint[:, tile:]
        hidden = gate_sum / (1.0 + jnp.exp(-gate_sum)) * up_sum * factor_ref[here, :]
        out_ref[here, :] = hidden.astype(jnp.bfloat16)


def up(index, tokens, tables, experts, pieces):
    rows, width_model = tokens[0].shape
    blocks = len(tokens)
    depth, joint_width = pieces[0][0].shape[1:]
    width = joint_width // 2
    tile = 256
    tiles = width // tile
    layout, operands, specs = [], [], []
    for offset in sorted(pieces):
        parts = pieces[offset]
        per = parts[0].shape[0]
        layout.append((offset, len(operands) // 2, per))
        for number, part in enumerate(parts):
            for side in range(2):

                def place(e, j, s, per=per, number=number, side=side):
                    if per > 1:
                        return e, 0, j + side * tiles
                    still = tiles - 1 if number == 0 else 0
                    return 0, 0, jnp.where(e == number, j, still) + side * tiles

                operands.append(part)
                specs.append(pl.BlockSpec((1, depth, tile), place))
    last = tables[0].shape[1] // LANES - 1
    return pl.pallas_call(
        functools.partial(up_kernel, layout, depth, experts, blocks),
        grid_spec=pltpu.PrefetchScalarGridSpec(
            num_scalar_prefetch=1,
            grid=(2, tiles),
            in_specs=[pl.BlockSpec((rows, width_model), lambda e, j, s: (0, 0))] * blocks
            + [pl.BlockSpec((rows, LANES), lambda e, j, s: (0, last))] * blocks
            + specs,
            out_specs=pl.BlockSpec((blocks * rows, tile), lambda e, j, s: (0, e * tiles + j)),
            scratch_shapes=[
                pltpu.VMEM((blocks * rows, width_model), jnp.bfloat16),
                pltpu.VMEM((blocks * rows, 1), jnp.float32),
                pltpu.VMEM((width_model, 2 * tile), jnp.bfloat16),
            ],
        ),
        out_shape=jax.ShapeDtypeStruct((blocks * rows, 2 * width), jnp.bfloat16),
        compiler_params=pltpu.CompilerParams(vmem_limit_bytes=MEMORY),
        cost_estimate=free(),
    )(index, *tokens, *tables, *operands)


def product(hidden, weights, part):
    first, second = weights[2 * part], weights[2 * part + 1]
    width = first.shape[2]
    return dot_nt(hidden[:, :width], first[0]) + dot_nt(hidden[:, width:], second[0])


def down_kernel(parts, *refs):
    hidden, weights, out_refs = refs[0], refs[1 : 1 + 2 * parts], refs[1 + 2 * parts :]
    for part in range(parts):
        out_refs[part][...] = product(hidden, weights, part).astype(jnp.bfloat16)


def down_add_kernel(parts, tile, *refs):
    hidden, weights, arrived = refs[0], refs[1 : 1 + 2 * parts], refs[1 + 2 * parts : 1 + 3 * parts]
    own_ref, *out_refs = refs[1 + 3 * parts :]
    rows, columns = own_ref.shape
    depth = columns // parts
    for part in range(parts):
        at = pl.ds(pl.multiple_of(part * depth + pl.program_id(0) * tile, tile), tile)
        out = product(hidden, weights, part) + arrived[part][...].astype(jnp.float32)
        own_ref[:, at] = out[:rows]
        for i, out_ref in enumerate(out_refs):
            out_ref[:, at] = out[(i + 1) * rows : (i + 2) * rows].astype(jnp.bfloat16)


def whole(*shape):
    return pl.BlockSpec(shape, lambda *i: (0,) * len(shape))


def down_operands(hidden, pieces, side):
    total_rows = hidden.shape[0]
    depth, width = pieces[0][0].shape[1:]
    tile = min(256, depth)
    specs = [pl.BlockSpec((total_rows // CORES, hidden.shape[1]), lambda i: (side, 0))]
    operands = [hidden]
    for parts in pieces:
        per = parts[0].shape[0]
        for expert in range(2):
            specs.append(
                pl.BlockSpec((1, tile, width), lambda i, at=expert % per: (at, i, 0))
            )
            operands.append(parts[expert // per])
    params = pltpu.CompilerParams(vmem_limit_bytes=MEMORY)
    options = dict(grid=(depth // tile,), compiler_params=params, cost_estimate=free())
    return specs, operands, options, tile, depth


def down_first(hidden, pieces, blocks):
    specs, operands, options, tile, depth = down_operands(hidden, pieces, 1)
    rows = hidden.shape[0] // CORES
    return pl.pallas_call(
        functools.partial(down_kernel, len(pieces)),
        in_specs=specs,
        out_specs=[pl.BlockSpec((rows, tile), lambda i: (0, i))] * len(pieces),
        out_shape=[jax.ShapeDtypeStruct((rows, depth), jnp.bfloat16)] * len(pieces),
        **options,
    )(*operands)


def down_second(hidden, pieces, blocks, arrived):
    specs, operands, options, tile, depth = down_operands(hidden, pieces, 0)
    rows, columns = hidden.shape[0] // blocks, depth * len(pieces)
    turns = blocks // CORES
    return pl.pallas_call(
        functools.partial(down_add_kernel, len(pieces), tile),
        in_specs=specs
        + [pl.BlockSpec((turns * rows, tile), lambda i: (0, i))] * len(pieces),
        out_specs=[whole(rows, columns)] * turns,
        out_shape=[jax.ShapeDtypeStruct((rows, columns), jnp.float32)]
        + [jax.ShapeDtypeStruct((rows, columns), jnp.bfloat16)] * (turns - 1),
        **options,
    )(*operands, *arrived)


def down_and_return(hidden, pieces, blocks):
    turns = blocks // CORES
    arrived = [flip(part, "ctx", 1) for part in down_first(hidden, pieces, blocks)]
    own, *sent = down_second(hidden, pieces, blocks, arrived)
    home = [turn(sent[d - 1], turns - d) for d in range(1, turns)]
    total = own
    for block in home:
        total += block.astype(jnp.float32)
    return total.astype(jnp.bfloat16), sent


def per_device(
    inputs,
    queries,
    kv_down,
    latent_gain,
    kv_up,
    out_proj,
    post_gain,
    expert_ids,
    gates,
    gate_up,
    down_proj,
):
    tokens = inputs[0]
    rows, width_model = tokens.shape
    ctx_size = lax.axis_size("ctx")
    rank = lax.axis_index("ctx")
    here = lax.axis_index("fsdp")
    turns = ctx_size // CORES
    local_experts = gate_up.shape[0]
    experts = local_experts * ctx_size

    up_pieces = first_step(gate_up)

    row_iota = jnp.arange(rows, dtype=jnp.int32)
    positions = rank * rows + row_iota
    cosine, sine = swing_tables(positions)
    cache = compress(
        tokens, kv_down, latent_gain, cosine, sine, expert_ids[0].T, gates[0].T, experts
    )
    mine = [cache] + [turn(cache, d) for d in range(1, turns)]
    z = rank // CORES
    core = rank % CORES
    owners = jnp.stack(
        [(z - d) % turns * CORES + side for d in range(turns) for side in (core, 1 - core)]
    )
    key_pos = (owners[:, None] * rows + row_iota[None, :]).reshape(1, -1)
    row_pos = positions[:, None]
    post_gain = post_gain[None, :]
    ready = [after(cached, key_pos, row_pos, post_gain) for cached in mine[1:]]
    keys = [block for held in (cache, *ready) for block in (held, flip(held, "ctx", 1))]
    attn_out, routed = attend(
        queries[0],
        kv_up,
        keys,
        key_pos,
        row_pos,
        cosine,
        sine,
        out_proj,
        tokens,
        post_gain,
    )

    near = (1, turns - 1)
    mine = {0: routed, **{d: turn(routed, d) for d in near}}
    up_pieces = {o: [after(p[0], *[mine[d] for d in near])] for o, p in up_pieces.items()}
    up_far, up_halves = second_step(up_pieces)
    late = after(routed, *up_halves) if up_halves else routed
    mine.update({d: turn(late, d) for d in range(1, turns) if d not in near})
    mine = [mine[d] for d in range(turns)]
    gathered = [block for held in mine for block in (held, flip(held, "ctx", 1))]
    last_up = [p for o in sorted(up_far) for p in up_far[o]]
    down_pieces = first_step(after(down_proj, *last_up, *gathered))
    index = jnp.stack([here, rank * local_experts]).astype(jnp.int32)
    up_pieces = {**up_pieces, **up_far}
    hidden = up(index, gathered, keys, experts, up_pieces)
    depth = down_proj.shape[1]
    moe = jnp.zeros((rows, width_model), jnp.bfloat16)
    groups = [(0,), (1, 2), None]
    earlier = []
    for offsets in groups:
        if offsets is None:
            offsets = tuple(sorted(down_far))
        held = after(hidden, *earlier) if earlier else hidden
        pieces = [down_pieces[offset] for offset in offsets]
        owned, earlier = down_and_return(held, pieces, ctx_size)
        if offsets == (0,):
            down_pieces = {o: [after(p[0], *earlier)] for o, p in down_pieces.items()}
            down_far, down_halves = second_step(down_pieces)
            down_pieces.update(down_far)
            earlier = [*earlier, *down_halves]
        for part, offset in enumerate(offsets):
            columns = owned[:, part * depth : (part + 1) * depth]
            start = jnp.bitwise_xor(here, offset) * depth
            moe = lax.dynamic_update_slice(moe, columns, (0, start))
    return (attn_out[None], moe[None])


def solution(mesh):
    in_specs = (
        P("fsdp", "ctx", None),
        P("fsdp", "ctx", None),
        P(),
        P(),
        P(),
        P(),
        P(),
        P("fsdp", "ctx", None),
        P("fsdp", "ctx", None),
        P("ctx", "fsdp", None),
        P("ctx", "fsdp", None),
    )
    out_specs = (P("fsdp", "ctx", None), P("fsdp", "ctx", None))
    return jax.shard_map(
        per_device, mesh=mesh, in_specs=in_specs, out_specs=out_specs, check_vma=False
    )
```

```python
import functools
import math

import jax
import jax.numpy as jnp
from jax import lax
from jax.experimental import pallas as pl
from jax.experimental.pallas import tpu as pltpu
from jax.sharding import PartitionSpec as P

HEADS = 16
NOPE = 128
ROPE = 64
VDIM = 128
LANES = 128

EPSILON = 1e-06
NEG_LARGE = -1e30
CORES = 2
NT = (((1,), (1,)), ((), ()))
MEMORY = 56 * 2**20
CHUNK = 512


def dot(left, right):
    return jnp.dot(left, right, preferred_element_type=jnp.float32)


def dot_nt(left, right):
    return lax.dot_general(left, right, NT, preferred_element_type=jnp.float32)


def free():
    return pl.CostEstimate(flops=0, bytes_accessed=0, transcendentals=0)


def normalize(values, gain):
    mean_sq = jnp.mean(values * values, axis=-1, keepdims=True)
    return values * lax.rsqrt(mean_sq + EPSILON) * gain


def swing_tables(positions):
    half = ROPE // 2
    lane = jnp.arange(LANES, dtype=jnp.int32)
    turn_of = (lane % half).astype(jnp.float32)
    freqs = jnp.exp(-(2.0 * turn_of / ROPE) * math.log(10000.0))
    angles = positions.astype(jnp.float32)[:, None] * freqs[None, :]
    cosine = jnp.where(lane < ROPE, jnp.cos(angles), 0.0)
    sine = jnp.where(lane < half, -jnp.sin(angles), jnp.where(lane < ROPE, jnp.sin(angles), 0.0))
    return cosine, sine


def swing(values, cosine, sine):
    half = ROPE // 2
    lane = lax.broadcasted_iota(jnp.int32, values.shape, 1)
    swapped = jnp.where(
        lane < half, pltpu.roll(values, LANES - half, 1), pltpu.roll(values, half, 1)
    )
    return values * cosine + swapped * sine


def flip(values, axis, mask):
    size = lax.axis_size(axis)
    return lax.ppermute(values, axis, [(i, i ^ mask) for i in range(size)])


def spread(held, bits):
    held = dict(held)
    for bit in bits:
        held.update({o | bit: flip(block, "ctx", bit) for o, block in list(held.items())})
    return held


def ctx_bits():
    size = lax.axis_size("ctx")
    return [1 << b for b in reversed(range(size.bit_length() - 1))]


def after(value, *earlier):
    return lax.optimization_barrier((value, *earlier))[0]


def first_step(shard):
    return {0: [shard], 1: [flip(shard, "fsdp", 1)], 2: [flip(shard, "fsdp", 2)]}


def second_step(pieces):
    size = lax.axis_size("fsdp")
    half = pieces[0][0].shape[0] // 2
    if size == 4:
        low_half, high_half = pieces[1][0][:half], pieces[2][0][half:]
        low = flip(low_half, "fsdp", 2)
        high = flip(high_half, "fsdp", 1)
        return {3: [low, high]}, [low_half, high_half]
    more = {3: [flip(pieces[1][0], "fsdp", 2)]}
    held = {**pieces, **more}
    bit = 4
    while bit < size:
        new = {o | bit: [flip(p[0], "fsdp", bit)] for o, p in held.items()}
        more.update(new)
        held.update(new)
        bit *= 2
    return more, []


def compress_kernel(
    experts, token_ref, kv_ref, gain_ref, cos_ref, sin_ref, ids_ref, gates_ref, out_ref, pad_ref
):
    width = gain_ref.shape[1]
    compressed = dot_nt(token_ref[...], kv_ref[...])
    latent = normalize(compressed[:, :width], gain_ref[...].astype(jnp.float32))
    out_ref[:, :width] = latent.astype(jnp.bfloat16)
    pad_ref[...] = jnp.zeros_like(pad_ref)
    pad_ref[:, :ROPE] = compressed[:, width:]
    swung = swing(pad_ref[...], cos_ref[...], sin_ref[...])
    lane = lax.broadcasted_iota(jnp.int32, swung.shape, 1)
    line = lax.broadcasted_iota(jnp.int32, swung.shape[::-1], 0)
    ids = ids_ref[...] + ROPE
    gates = gates_ref[...]
    table = jnp.zeros(line.shape, jnp.float32)
    for k in range(ids.shape[0]):
        pick = ids[k : k + 1, :]
        named = (pick == line) | (pick + experts == line)
        table += jnp.where(named, gates[k : k + 1, :], 0.0)
    table = table.T
    high = table.astype(jnp.bfloat16).astype(jnp.float32)
    table = jnp.where(lane < ROPE + experts, high, table - high)
    out_ref[:, width:] = jnp.where(lane < ROPE, swung, table).astype(jnp.bfloat16)


def compress(tokens, kv_down, latent_gain, cosine, sine, ids, gates, experts):
    rows = tokens.shape[0]
    return pl.pallas_call(
        functools.partial(compress_kernel, experts),
        out_shape=jax.ShapeDtypeStruct((rows, latent_gain.shape[0] + LANES), jnp.bfloat16),
        scratch_shapes=[pltpu.VMEM((rows, LANES), jnp.float32)],
        compiler_params=pltpu.CompilerParams(vmem_limit_bytes=MEMORY),
        cost_estimate=free(),
    )(tokens, kv_down.T, latent_gain[None, :], cosine, sine, ids, gates)


def attend_kernel(
    pairs,
    blocks,
    query_ref,
    up_ref,
    key_pos_ref,
    row_pos_ref,
    cos_ref,
    sin_ref,
    out_proj_ref,
    token_ref,
    gain_ref,
    *refs,
):
    key_refs = refs[:blocks]
    attn_ref, routed_ref, acc_ref, packed_ref, bias_ref, keys_ref, turned_ref = refs[blocks:]
    rows = token_ref.shape[0]
    latent_width = up_ref.shape[0]
    head_width = NOPE + VDIM
    scale = (NOPE + ROPE) ** (-0.5)
    step = pl.program_id(0)

    @pl.when(step == 0)
    def _():
        acc_ref[...] = jnp.zeros_like(acc_ref)
        bias_ref[...] = jnp.where(key_pos_ref[...] <= row_pos_ref[...], 0.0, NEG_LARGE)
        for i, ref in enumerate(key_refs):
            keys_ref[i * rows : (i + 1) * rows, :] = ref[...]
            turned_ref[:, i * rows : (i + 1) * rows] = ref[...].T

    cosine, sine = cos_ref[...], sin_ref[...]
    lane = lax.broadcasted_iota(jnp.int32, (rows, LANES), 1)
    for pair in range(pairs):
        base = pair * 2 * (NOPE + ROPE)
        middle = query_ref[:, base + LANES : base + 2 * LANES].astype(jnp.float32)
        last = query_ref[:, base + 2 * LANES : base + 3 * LANES].astype(jnp.float32)
        middle_back, last_back = pltpu.roll(middle, ROPE, 1), pltpu.roll(last, ROPE, 1)
        plain = (
            query_ref[:, base : base + LANES],
            jnp.where(lane < ROPE, middle_back, last_back).astype(jnp.bfloat16),
        )
        turned = (middle, last_back)
        for h in range(2):
            at = (pair * 2 + h) * head_width
            here = slice((pair * 2 + h) * rows, (pair * 2 + h + 1) * rows)
            absorbed = dot_nt(plain[h], up_ref[:, at : at + NOPE])
            packed_ref[here, :latent_width] = (absorbed * scale).astype(jnp.bfloat16)
            swung = swing(turned[h], cosine, sine)
            packed_ref[here, latent_width:] = (swung * scale).astype(jnp.bfloat16)
        packed = packed_ref[pair * 2 * rows : (pair + 1) * 2 * rows, :]
        scores = dot(packed, turned_ref[...])
        bias = bias_ref[...]
        scores = scores + jnp.concatenate([bias, bias], axis=0)
        expo = jnp.exp(scores - jnp.max(scores, axis=1, keepdims=True))
        total = jnp.sum(expo, axis=1, keepdims=True)
        context = dot(expo.astype(jnp.bfloat16), keys_ref[:, :latent_width])
        context = (context / total).astype(jnp.bfloat16)
        heads = []
        for h in range(2):
            at = (pair * 2 + h) * head_width + NOPE
            heads.append(dot(context[h * rows : (h + 1) * rows], up_ref[:, at : at + VDIM]))
        heads = jnp.concatenate(heads, axis=1).astype(jnp.bfloat16)
        acc_ref[...] += dot(heads, out_proj_ref[pair * 2 * VDIM : (pair + 1) * 2 * VDIM, :])

    @pl.when(step == pl.num_programs(0) - 1)
    def _():
        attn = acc_ref[...]
        attn_ref[...] = attn.astype(jnp.bfloat16)
        routed = normalize(
            token_ref[...].astype(jnp.float32) + attn, gain_ref[...].astype(jnp.float32)
        )
        routed_ref[...] = routed.astype(jnp.bfloat16)


def attend(queries, kv_up, keys, key_pos, row_pos, cosine, sine, out_proj, tokens, post_gain):
    rows, width_model = tokens.shape
    pairs = 2
    steps = HEADS // (2 * pairs)
    latent_width = kv_up.shape[0]
    key_width = keys[0].shape[1]
    count = key_pos.shape[1]

    def whole(*shape):
        return pl.BlockSpec(shape, lambda i: (0, 0))

    return pl.pallas_call(
        functools.partial(attend_kernel, pairs, len(keys)),
        grid=(steps,),
        in_specs=[
            pl.BlockSpec((rows, pairs * 2 * (NOPE + ROPE)), lambda i: (0, i)),
            pl.BlockSpec((latent_width, pairs * 2 * (NOPE + VDIM)), lambda i: (0, i)),
            whole(1, count),
            whole(rows, 1),
            whole(rows, LANES),
            whole(rows, LANES),
            pl.BlockSpec((pairs * 2 * VDIM, width_model), lambda i: (i, 0)),
            whole(rows, width_model),
            whole(1, width_model),
        ]
        + [whole(rows, key_width)] * len(keys),
        out_specs=[whole(rows, width_model)] * 2,
        out_shape=[jax.ShapeDtypeStruct((rows, width_model), jnp.bfloat16)] * 2,
        scratch_shapes=[
            pltpu.VMEM((rows, width_model), jnp.float32),
            pltpu.VMEM((pairs * 2 * rows, key_width), jnp.bfloat16),
            pltpu.VMEM((rows, count), jnp.float32),
            pltpu.VMEM((count, key_width), jnp.bfloat16),
            pltpu.VMEM((key_width, count), jnp.bfloat16),
        ],
        compiler_params=pltpu.CompilerParams(vmem_limit_bytes=MEMORY),
        cost_estimate=free(),
    )(
        queries,
        kv_up,
        key_pos,
        row_pos,
        cosine,
        sine,
        out_proj,
        tokens,
        post_gain,
        *keys,
    )


def up_kernel(layout, depth, experts, blocks, index_ref, *refs):
    x_refs, table_refs = refs[:blocks], refs[blocks : 2 * blocks]
    weights = refs[2 * blocks : -4]
    out_ref, x_ref, factor_ref, w_ref = refs[-4:]
    expert = pl.program_id(0)
    me = index_ref[0]
    named = index_ref[1] + expert + ROPE
    rows = x_refs[0].shape[0]
    tile = out_ref.shape[1]

    @pl.when((expert == 0) & (pl.program_id(1) == 0))
    def _():
        for i in range(blocks):
            place = (i % CORES) * (blocks // CORES) + i // CORES
            here = slice(place * rows, (place + 1) * rows)
            for part, (offset, _, _) in enumerate(layout):
                at = pl.ds(pl.multiple_of(jnp.bitwise_xor(me, offset) * depth, depth), depth)
                x_ref[here, part * depth : (part + 1) * depth] = x_refs[i][:, at]

    @pl.when(pl.program_id(1) == 0)
    def _():
        for i in range(blocks):
            place = (i % CORES) * (blocks // CORES) + i // CORES
            here = slice(place * rows, (place + 1) * rows)
            table = table_refs[i][...].astype(jnp.float32)
            lane = lax.broadcasted_iota(jnp.int32, table.shape, 1)
            mine = (lane == named) | (lane == named + experts)
            factor_ref[here, :] = jnp.sum(jnp.where(mine, table, 0.0), axis=1, keepdims=True)

    for part, (_, first, per) in enumerate(layout):
        here = slice(part * depth, (part + 1) * depth)

        def fill(at, here=here):
            w_ref[here, :tile] = weights[2 * at][0]
            w_ref[here, tile:] = weights[2 * at + 1][0]

        if per > 1:
            fill(first)
        else:
            pl.when(expert == 0)(functools.partial(fill, first))
            pl.when(expert == 1)(functools.partial(fill, first + 1))
    step = min(CHUNK, blocks * rows)
    for start in range(0, blocks * rows, step):
        here = slice(start, start + step)
        joint = dot(x_ref[here, :], w_ref[...])
        gate_sum, up_sum = joint[:, :tile], joint[:, tile:]
        hidden = gate_sum / (1.0 + jnp.exp(-gate_sum)) * up_sum * factor_ref[here, :]
        out_ref[here, :] = hidden.astype(jnp.bfloat16)


def up(index, tokens, tables, experts, pieces):
    rows, width_model = tokens[0].shape
    blocks = len(tokens)
    depth, joint_width = pieces[0][0].shape[1:]
    width = joint_width // 2
    tile = 256
    tiles = width // tile
    layout, operands, specs = [], [], []
    for offset in sorted(pieces):
        parts = pieces[offset]
        per = parts[0].shape[0]
        layout.append((offset, len(operands) // 2, per))
        for number, part in enumerate(parts):
            for side in range(2):

                def place(e, j, s, per=per, number=number, side=side):
                    if per > 1:
                        return e, 0, j + side * tiles
                    still = tiles - 1 if number == 0 else 0
                    return 0, 0, jnp.where(e == number, j, still) + side * tiles

                operands.append(part)
                specs.append(pl.BlockSpec((1, depth, tile), place))
    last = tables[0].shape[1] // LANES - 1
    return pl.pallas_call(
        functools.partial(up_kernel, layout, depth, experts, blocks),
        grid_spec=pltpu.PrefetchScalarGridSpec(
            num_scalar_prefetch=1,
            grid=(2, tiles),
            in_specs=[pl.BlockSpec((rows, width_model), lambda e, j, s: (0, 0))] * blocks
            + [pl.BlockSpec((rows, LANES), lambda e, j, s: (0, last))] * blocks
            + specs,
            out_specs=pl.BlockSpec((blocks * rows, tile), lambda e, j, s: (0, e * tiles + j)),
            scratch_shapes=[
                pltpu.VMEM((blocks * rows, width_model), jnp.bfloat16),
                pltpu.VMEM((blocks * rows, 1), jnp.float32),
                pltpu.VMEM((width_model, 2 * tile), jnp.bfloat16),
            ],
        ),
        out_shape=jax.ShapeDtypeStruct((blocks * rows, 2 * width), jnp.bfloat16),
        compiler_params=pltpu.CompilerParams(vmem_limit_bytes=MEMORY),
        cost_estimate=free(),
    )(index, *tokens, *tables, *operands)


def product(hidden, weights, part):
    first, second = weights[2 * part], weights[2 * part + 1]
    width = first.shape[2]
    return dot_nt(hidden[:, :width], first[0]) + dot_nt(hidden[:, width:], second[0])


def down_kernel(parts, *refs):
    hidden, weights, out_refs = refs[0], refs[1 : 1 + 2 * parts], refs[1 + 2 * parts :]
    for part in range(parts):
        out_refs[part][...] = product(hidden, weights, part).astype(jnp.bfloat16)


def down_add_kernel(parts, tile, *refs):
    hidden, weights, arrived = refs[0], refs[1 : 1 + 2 * parts], refs[1 + 2 * parts : 1 + 3 * parts]
    kept_ref, sent_ref, sum_ref = refs[1 + 3 * parts :]
    count, rows, columns = kept_ref.shape
    depth = columns // parts
    for part in range(parts):
        at = pl.ds(pl.multiple_of(part * depth + pl.program_id(0) * tile, tile), tile)
        sum_ref[...] = product(hidden, weights, part) + arrived[part][...].astype(jnp.float32)
        for i in range(count):
            kept_ref[i, :, at] = sum_ref[2 * i * rows : (2 * i + 1) * rows, :]
            sent = sum_ref[(2 * i + 1) * rows : (2 * i + 2) * rows, :]
            sent_ref[i, :, at] = sent.astype(jnp.bfloat16)


def whole(*shape):
    return pl.BlockSpec(shape, lambda *i: (0,) * len(shape))


def down_operands(hidden, pieces, side):
    total_rows = hidden.shape[0]
    depth, width = pieces[0][0].shape[1:]
    tile = min(256, depth)
    specs = [pl.BlockSpec((total_rows // CORES, hidden.shape[1]), lambda i: (side, 0))]
    operands = [hidden]
    for parts in pieces:
        per = parts[0].shape[0]
        for expert in range(2):
            specs.append(
                pl.BlockSpec((1, tile, width), lambda i, at=expert % per: (at, i, 0))
            )
            operands.append(parts[expert // per])
    params = pltpu.CompilerParams(vmem_limit_bytes=MEMORY)
    options = dict(grid=(depth // tile,), compiler_params=params, cost_estimate=free())
    return specs, operands, options, tile, depth


def down_first(hidden, pieces, blocks):
    specs, operands, options, tile, depth = down_operands(hidden, pieces, 1)
    rows = hidden.shape[0] // CORES
    return pl.pallas_call(
        functools.partial(down_kernel, len(pieces)),
        in_specs=specs,
        out_specs=[pl.BlockSpec((rows, tile), lambda i: (0, i))] * len(pieces),
        out_shape=[jax.ShapeDtypeStruct((rows, depth), jnp.bfloat16)] * len(pieces),
        **options,
    )(*operands)


def down_second(hidden, pieces, blocks, arrived):
    specs, operands, options, tile, depth = down_operands(hidden, pieces, 0)
    shape = (blocks // 4, hidden.shape[0] // blocks, depth * len(pieces))
    half = hidden.shape[0] // CORES
    return pl.pallas_call(
        functools.partial(down_add_kernel, len(pieces), tile),
        in_specs=specs + [pl.BlockSpec((half, tile), lambda i: (0, i))] * len(pieces),
        out_specs=[whole(*shape)] * 2,
        out_shape=[
            jax.ShapeDtypeStruct(shape, jnp.float32),
            jax.ShapeDtypeStruct(shape, jnp.bfloat16),
        ],
        scratch_shapes=[pltpu.VMEM((half, tile), jnp.float32)],
        **options,
    )(*operands, *arrived)


def down_and_return(hidden, pieces, blocks):
    arrived = [flip(part, "ctx", 1) for part in down_first(hidden, pieces, blocks)]
    kept, sent = down_second(hidden, pieces, blocks, arrived)
    first_sent = sent
    bit = 2
    while True:
        home = flip(sent, "ctx", bit)
        if kept.shape[0] == 1:
            return kept[0], home[0], first_sent
        total = kept + home.astype(jnp.float32)
        total = total.reshape(total.shape[0] // 2, 2, *total.shape[1:])
        kept, sent = total[:, 0], total[:, 1].astype(jnp.bfloat16)
        bit *= 2


def per_device(
    inputs,
    queries,
    kv_down,
    latent_gain,
    kv_up,
    out_proj,
    post_gain,
    expert_ids,
    gates,
    gate_up,
    down_proj,
):
    tokens = inputs[0]
    rows, width_model = tokens.shape
    ctx_size = lax.axis_size("ctx")
    rank = lax.axis_index("ctx")
    here = lax.axis_index("fsdp")
    local_experts = gate_up.shape[0]
    experts = local_experts * ctx_size

    up_pieces = first_step(gate_up)

    row_iota = jnp.arange(rows, dtype=jnp.int32)
    positions = rank * rows + row_iota
    cosine, sine = swing_tables(positions)
    cache = compress(
        tokens, kv_down, latent_gain, cosine, sine, expert_ids[0].T, gates[0].T, experts
    )
    bits = ctx_bits()
    held = spread({0: cache}, bits[:-1])
    owners = jnp.bitwise_xor(rank, jnp.arange(ctx_size, dtype=jnp.int32))
    key_pos = (owners[:, None] * rows + row_iota[None, :]).reshape(1, -1)
    row_pos = positions[:, None]
    post_gain = post_gain[None, :]
    held = {o: after(block, key_pos, row_pos, post_gain) if o else block for o, block in held.items()}
    held = spread(held, bits[-1:])
    keys = [held[o] for o in range(ctx_size)]
    attn_out, routed = attend(
        queries[0],
        kv_up,
        keys,
        key_pos,
        row_pos,
        cosine,
        sine,
        out_proj,
        tokens,
        post_gain,
    )

    held = spread({0: routed}, bits[:1])
    up_pieces = {o: [after(p[0], held[bits[0]])] for o, p in up_pieces.items()}
    up_far, up_halves = second_step(up_pieces)
    held = {o: after(block, *up_halves) for o, block in held.items()} if up_halves else held
    held = spread(held, bits[1:])
    gathered = [held[o] for o in range(ctx_size)]
    last_up = [p for o in sorted(up_far) for p in up_far[o]]
    down_pieces = first_step(after(down_proj, *last_up, *gathered))
    index = jnp.stack([here, rank * local_experts]).astype(jnp.int32)
    up_pieces = {**up_pieces, **up_far}
    hidden = up(index, gathered, keys, experts, up_pieces)
    depth = down_proj.shape[1]
    moe = jnp.zeros((rows, width_model), jnp.bfloat16)
    groups = [(0,), (1, 2), None]
    returned = []
    earlier = []
    for offsets in groups:
        if offsets is None:
            offsets = tuple(sorted(down_far))
        held = after(hidden, *earlier) if earlier else hidden
        pieces = [down_pieces[offset] for offset in offsets]
        own, home, sent = down_and_return(held, pieces, ctx_size)
        earlier = [sent]
        if offsets == (1, 2):
            earlier = [earlier[0], returned[0][2]]
        returned.append((offsets, own, home))
        if offsets == (0,):
            down_pieces = {o: [after(p[0], *earlier)] for o, p in down_pieces.items()}
            down_far, down_halves = second_step(down_pieces)
            down_pieces.update(down_far)
            earlier = [*earlier, *down_halves]
    for offsets, own, home in returned:
        if offsets == (1, 2):
            home = after(home, *earlier)
        own += home.astype(jnp.float32)
        owned = own.astype(jnp.bfloat16)
        for part, offset in enumerate(offsets):
            columns = owned[:, part * depth : (part + 1) * depth]
            start = jnp.bitwise_xor(here, offset) * depth
            moe = lax.dynamic_update_slice(moe, columns, (0, start))
    return (attn_out[None], moe[None])


def solution(mesh):
    in_specs = (
        P("fsdp", "ctx", None),
        P("fsdp", "ctx", None),
        P(),
        P(),
        P(),
        P(),
        P(),
        P("fsdp", "ctx", None),
        P("fsdp", "ctx", None),
        P("ctx", "fsdp", None),
        P("ctx", "fsdp", None),
    )
    out_specs = (P("fsdp", "ctx", None), P("fsdp", "ctx", None))
    return jax.shard_map(
        per_device, mesh=mesh, in_specs=in_specs, out_specs=out_specs, check_vma=False
    )
```

```python
import functools
import math

import jax
import jax.numpy as jnp
from jax import lax
from jax.experimental import pallas as pl
from jax.experimental.pallas import tpu as pltpu
from jax.sharding import PartitionSpec as P

HEADS = 16
NOPE = 128
ROPE = 64
VDIM = 128
LANES = 128

EPSILON = 1e-06
NEG_LARGE = -1e30
CORES = 2
NT = (((1,), (1,)), ((), ()))
MEMORY = 56 * 2**20
CHUNK = 512


def dot(left, right):
    return jnp.dot(left, right, preferred_element_type=jnp.float32)


def dot_nt(left, right):
    return lax.dot_general(left, right, NT, preferred_element_type=jnp.float32)


def free():
    return pl.CostEstimate(flops=0, bytes_accessed=0, transcendentals=0)


def normalize(values, gain):
    mean_sq = jnp.mean(values * values, axis=-1, keepdims=True)
    return values * lax.rsqrt(mean_sq + EPSILON) * gain


def swing_tables(positions):
    half = ROPE // 2
    lane = jnp.arange(LANES, dtype=jnp.int32)
    turn_of = (lane % half).astype(jnp.float32)
    freqs = jnp.exp(-(2.0 * turn_of / ROPE) * math.log(10000.0))
    angles = positions.astype(jnp.float32)[:, None] * freqs[None, :]
    cosine = jnp.where(lane < ROPE, jnp.cos(angles), 0.0)
    sine = jnp.where(lane < half, -jnp.sin(angles), jnp.where(lane < ROPE, jnp.sin(angles), 0.0))
    return cosine, sine


def swing(values, cosine, sine):
    half = ROPE // 2
    lane = lax.broadcasted_iota(jnp.int32, values.shape, 1)
    swapped = jnp.where(
        lane < half, pltpu.roll(values, LANES - half, 1), pltpu.roll(values, half, 1)
    )
    return values * cosine + swapped * sine


def flip(values, axis, mask):
    size = lax.axis_size(axis)
    return lax.ppermute(values, axis, [(i, i ^ mask) for i in range(size)])


def spread(held, bits):
    held = dict(held)
    for bit in bits:
        held.update({o | bit: flip(block, "ctx", bit) for o, block in list(held.items())})
    return held


def ctx_bits():
    size = lax.axis_size("ctx")
    return [1 << b for b in reversed(range(size.bit_length() - 1))]


def after(value, *earlier):
    return lax.optimization_barrier((value, *earlier))[0]


def first_step(shard):
    return {0: [shard], 1: [flip(shard, "fsdp", 1)], 2: [flip(shard, "fsdp", 2)]}


def second_step(pieces):
    size = lax.axis_size("fsdp")
    half = pieces[0][0].shape[0] // 2
    if size == 4:
        low_half, high_half = pieces[1][0][:half], pieces[2][0][half:]
        low = flip(low_half, "fsdp", 2)
        high = flip(high_half, "fsdp", 1)
        return {3: [low, high]}, [low_half, high_half]
    more = {3: [flip(pieces[1][0], "fsdp", 2)]}
    held = {**pieces, **more}
    bit = 4
    while bit < size:
        new = {o | bit: [flip(p[0], "fsdp", bit)] for o, p in held.items()}
        more.update(new)
        held.update(new)
        bit *= 2
    return more, []


def pick_major(values):
    return jnp.transpose(values, (2, 0, 1))


def compress_kernel(
    experts, token_ref, kv_ref, gain_ref, cos_ref, sin_ref, ids_ref, gates_ref, out_ref, pad_ref
):
    width = gain_ref.shape[0]
    compressed = dot_nt(token_ref[...], kv_ref[...])
    latent = normalize(compressed[:, :width], gain_ref[...].astype(jnp.float32)[None, :])
    out_ref[:, :width] = latent.astype(jnp.bfloat16)
    pad_ref[...] = jnp.zeros_like(pad_ref)
    pad_ref[:, :ROPE] = compressed[:, width:]
    swung = swing(pad_ref[...], cos_ref[...], sin_ref[...])
    lane = lax.broadcasted_iota(jnp.int32, swung.shape, 1)
    line = lax.broadcasted_iota(jnp.int32, swung.shape[::-1], 0)
    table = jnp.zeros(line.shape, jnp.float32)
    for k in range(ids_ref.shape[0]):
        pick = ids_ref[k] + ROPE
        named = (pick == line) | (pick + experts == line)
        table += jnp.where(named, gates_ref[k], 0.0)
    table = table.T
    high = table.astype(jnp.bfloat16).astype(jnp.float32)
    table = jnp.where(lane < ROPE + experts, high, table - high)
    out_ref[:, width:] = jnp.where(lane < ROPE, swung, table).astype(jnp.bfloat16)


def compress(tokens, kv_down, latent_gain, cosine, sine, ids, gates, experts):
    rows = tokens.shape[0]
    return pl.pallas_call(
        functools.partial(compress_kernel, experts),
        out_shape=jax.ShapeDtypeStruct((rows, latent_gain.shape[0] + LANES), jnp.bfloat16),
        scratch_shapes=[pltpu.VMEM((rows, LANES), jnp.float32)],
        compiler_params=pltpu.CompilerParams(vmem_limit_bytes=MEMORY),
        cost_estimate=free(),
    )(tokens, kv_down.T, latent_gain, cosine, sine, ids, gates)


def attend_kernel(
    pairs,
    blocks,
    query_ref,
    up_ref,
    key_pos_ref,
    row_pos_ref,
    cos_ref,
    sin_ref,
    out_proj_ref,
    token_ref,
    gain_ref,
    *refs,
):
    key_refs = refs[:blocks]
    attn_ref, routed_ref, acc_ref, packed_ref, bias_ref, keys_ref, turned_ref = refs[blocks:]
    rows = token_ref.shape[0]
    latent_width = up_ref.shape[0]
    head_width = NOPE + VDIM
    scale = (NOPE + ROPE) ** (-0.5)
    step = pl.program_id(0)

    @pl.when(step == 0)
    def _():
        acc_ref[...] = jnp.zeros_like(acc_ref)
        bias_ref[...] = jnp.where(key_pos_ref[...] <= row_pos_ref[...], 0.0, NEG_LARGE)
        for i, ref in enumerate(key_refs):
            keys_ref[i * rows : (i + 1) * rows, :] = ref[...]
            turned_ref[:, i * rows : (i + 1) * rows] = ref[...].T

    cosine, sine = cos_ref[...], sin_ref[...]
    lane = lax.broadcasted_iota(jnp.int32, (rows, LANES), 1)
    for pair in range(pairs):
        base = pair * 2 * (NOPE + ROPE)
        middle = query_ref[:, base + LANES : base + 2 * LANES].astype(jnp.float32)
        last = query_ref[:, base + 2 * LANES : base + 3 * LANES].astype(jnp.float32)
        middle_back, last_back = pltpu.roll(middle, ROPE, 1), pltpu.roll(last, ROPE, 1)
        plain = (
            query_ref[:, base : base + LANES],
            jnp.where(lane < ROPE, middle_back, last_back).astype(jnp.bfloat16),
        )
        turned = (middle, last_back)
        for h in range(2):
            at = (pair * 2 + h) * head_width
            here = slice((pair * 2 + h) * rows, (pair * 2 + h + 1) * rows)
            absorbed = dot_nt(plain[h], up_ref[:, at : at + NOPE])
            packed_ref[here, :latent_width] = (absorbed * scale).astype(jnp.bfloat16)
            swung = swing(turned[h], cosine, sine)
            packed_ref[here, latent_width:] = (swung * scale).astype(jnp.bfloat16)
        packed = packed_ref[pair * 2 * rows : (pair + 1) * 2 * rows, :]
        scores = dot(packed, turned_ref[...])
        bias = bias_ref[...]
        scores = scores + jnp.concatenate([bias, bias], axis=0)
        expo = jnp.exp(scores - jnp.max(scores, axis=1, keepdims=True))
        total = jnp.sum(expo, axis=1, keepdims=True)
        context = dot(expo.astype(jnp.bfloat16), keys_ref[:, :latent_width])
        context = (context / total).astype(jnp.bfloat16)
        heads = []
        for h in range(2):
            at = (pair * 2 + h) * head_width + NOPE
            heads.append(dot(context[h * rows : (h + 1) * rows], up_ref[:, at : at + VDIM]))
        heads = jnp.concatenate(heads, axis=1).astype(jnp.bfloat16)
        acc_ref[...] += dot(heads, out_proj_ref[pair * 2 * VDIM : (pair + 1) * 2 * VDIM, :])

    @pl.when(step == pl.num_programs(0) - 1)
    def _():
        attn = acc_ref[...]
        attn_ref[...] = attn.astype(jnp.bfloat16)
        routed = normalize(
            token_ref[...].astype(jnp.float32) + attn, gain_ref[...].astype(jnp.float32)
        )
        routed_ref[...] = routed.astype(jnp.bfloat16)


def attend(queries, kv_up, keys, key_pos, row_pos, cosine, sine, out_proj, tokens, post_gain):
    rows, width_model = tokens.shape
    pairs = 2
    steps = HEADS // (2 * pairs)
    latent_width = kv_up.shape[0]
    key_width = keys[0].shape[1]
    count = key_pos.shape[1]

    def whole(*shape):
        return pl.BlockSpec(shape, lambda i: (0, 0))

    return pl.pallas_call(
        functools.partial(attend_kernel, pairs, len(keys)),
        grid=(steps,),
        in_specs=[
            pl.BlockSpec((rows, pairs * 2 * (NOPE + ROPE)), lambda i: (0, i)),
            pl.BlockSpec((latent_width, pairs * 2 * (NOPE + VDIM)), lambda i: (0, i)),
            whole(1, count),
            whole(rows, 1),
            whole(rows, LANES),
            whole(rows, LANES),
            pl.BlockSpec((pairs * 2 * VDIM, width_model), lambda i: (i, 0)),
            whole(rows, width_model),
            whole(1, width_model),
        ]
        + [whole(rows, key_width)] * len(keys),
        out_specs=[whole(rows, width_model)] * 2,
        out_shape=[jax.ShapeDtypeStruct((rows, width_model), jnp.bfloat16)] * 2,
        scratch_shapes=[
            pltpu.VMEM((rows, width_model), jnp.float32),
            pltpu.VMEM((pairs * 2 * rows, key_width), jnp.bfloat16),
            pltpu.VMEM((rows, count), jnp.float32),
            pltpu.VMEM((count, key_width), jnp.bfloat16),
            pltpu.VMEM((key_width, count), jnp.bfloat16),
        ],
        compiler_params=pltpu.CompilerParams(vmem_limit_bytes=MEMORY),
        cost_estimate=free(),
    )(
        queries,
        kv_up,
        key_pos,
        row_pos,
        cosine,
        sine,
        out_proj,
        tokens,
        post_gain,
        *keys,
    )


def up_kernel(layout, depth, experts, blocks, index_ref, *refs):
    x_refs, table_refs = refs[:blocks], refs[blocks : 2 * blocks]
    weights = refs[2 * blocks : -4]
    out_ref, x_ref, factor_ref, w_ref = refs[-4:]
    expert = pl.program_id(0)
    me = index_ref[0]
    named = index_ref[1] + expert + ROPE
    rows = x_refs[0].shape[0]
    tile = out_ref.shape[1]

    @pl.when((expert == 0) & (pl.program_id(1) == 0))
    def _():
        for i in range(blocks):
            place = (i % CORES) * (blocks // CORES) + i // CORES
            here = slice(place * rows, (place + 1) * rows)
            for part, (offset, _, _) in enumerate(layout):
                at = pl.ds(pl.multiple_of(jnp.bitwise_xor(me, offset) * depth, depth), depth)
                x_ref[here, part * depth : (part + 1) * depth] = x_refs[i][:, at]

    @pl.when(pl.program_id(1) == 0)
    def _():
        for i in range(blocks):
            place = (i % CORES) * (blocks // CORES) + i // CORES
            here = slice(place * rows, (place + 1) * rows)
            table = table_refs[i][...].astype(jnp.float32)
            lane = lax.broadcasted_iota(jnp.int32, table.shape, 1)
            mine = (lane == named) | (lane == named + experts)
            factor_ref[here, :] = jnp.sum(jnp.where(mine, table, 0.0), axis=1, keepdims=True)

    for part, (_, first, per) in enumerate(layout):
        here = slice(part * depth, (part + 1) * depth)

        def fill(at, here=here):
            w_ref[here, :tile] = weights[2 * at][0]
            w_ref[here, tile:] = weights[2 * at + 1][0]

        if per > 1:
            fill(first)
        else:
            pl.when(expert == 0)(functools.partial(fill, first))
            pl.when(expert == 1)(functools.partial(fill, first + 1))
    step = min(CHUNK, blocks * rows)
    for start in range(0, blocks * rows, step):
        here = slice(start, start + step)
        joint = dot(x_ref[here, :], w_ref[...])
        gate_sum, up_sum = joint[:, :tile], joint[:, tile:]
        hidden = gate_sum / (1.0 + jnp.exp(-gate_sum)) * up_sum * factor_ref[here, :]
        out_ref[here, :] = hidden.astype(jnp.bfloat16)


def up(index, tokens, tables, experts, pieces):
    rows, width_model = tokens[0].shape
    blocks = len(tokens)
    depth, joint_width = pieces[0][0].shape[1:]
    width = joint_width // 2
    tile = 256
    tiles = width // tile
    layout, operands, specs = [], [], []
    for offset in sorted(pieces):
        parts = pieces[offset]
        per = parts[0].shape[0]
        layout.append((offset, len(operands) // 2, per))
        for number, part in enumerate(parts):
            for side in range(2):

                def place(e, j, s, per=per, number=number, side=side):
                    if per > 1:
                        return e, 0, j + side * tiles
                    still = tiles - 1 if number == 0 else 0
                    return 0, 0, jnp.where(e == number, j, still) + side * tiles

                operands.append(part)
                specs.append(pl.BlockSpec((1, depth, tile), place))
    last = tables[0].shape[1] // LANES - 1
    return pl.pallas_call(
        functools.partial(up_kernel, layout, depth, experts, blocks),
        grid_spec=pltpu.PrefetchScalarGridSpec(
            num_scalar_prefetch=1,
            grid=(2, tiles),
            in_specs=[pl.BlockSpec((rows, width_model), lambda e, j, s: (0, 0))] * blocks
            + [pl.BlockSpec((rows, LANES), lambda e, j, s: (0, last))] * blocks
            + specs,
            out_specs=pl.BlockSpec((blocks * rows, tile), lambda e, j, s: (0, e * tiles + j)),
            scratch_shapes=[
                pltpu.VMEM((blocks * rows, width_model), jnp.bfloat16),
                pltpu.VMEM((blocks * rows, 1), jnp.float32),
                pltpu.VMEM((width_model, 2 * tile), jnp.bfloat16),
            ],
        ),
        out_shape=jax.ShapeDtypeStruct((blocks * rows, 2 * width), jnp.bfloat16),
        compiler_params=pltpu.CompilerParams(vmem_limit_bytes=MEMORY),
        cost_estimate=free(),
    )(index, *tokens, *tables, *operands)


def product(hidden, weights, part):
    first, second = weights[2 * part], weights[2 * part + 1]
    width = first.shape[2]
    return dot_nt(hidden[:, :width], first[0]) + dot_nt(hidden[:, width:], second[0])


def down_kernel(parts, *refs):
    hidden, weights, out_refs = refs[0], refs[1 : 1 + 2 * parts], refs[1 + 2 * parts :]
    for part in range(parts):
        out_refs[part][...] = product(hidden, weights, part).astype(jnp.bfloat16)


def down_add_kernel(parts, tile, *refs):
    hidden, weights, arrived = refs[0], refs[1 : 1 + 2 * parts], refs[1 + 2 * parts : 1 + 3 * parts]
    kept_ref, sent_ref, sum_ref = refs[1 + 3 * parts :]
    count, rows, columns = kept_ref.shape
    depth = columns // parts
    for part in range(parts):
        at = pl.ds(pl.multiple_of(part * depth + pl.program_id(0) * tile, tile), tile)
        sum_ref[...] = product(hidden, weights, part) + arrived[part][...].astype(jnp.float32)
        for i in range(count):
            kept_ref[i, :, at] = sum_ref[2 * i * rows : (2 * i + 1) * rows, :]
            sent = sum_ref[(2 * i + 1) * rows : (2 * i + 2) * rows, :]
            sent_ref[i, :, at] = sent.astype(jnp.bfloat16)


def whole(*shape):
    return pl.BlockSpec(shape, lambda *i: (0,) * len(shape))


def down_operands(hidden, pieces, side):
    total_rows = hidden.shape[0]
    depth, width = pieces[0][0].shape[1:]
    tile = min(256, depth)
    specs = [pl.BlockSpec((total_rows // CORES, hidden.shape[1]), lambda i: (side, 0))]
    operands = [hidden]
    for parts in pieces:
        per = parts[0].shape[0]
        for expert in range(2):
            specs.append(
                pl.BlockSpec((1, tile, width), lambda i, at=expert % per: (at, i, 0))
            )
            operands.append(parts[expert // per])
    params = pltpu.CompilerParams(vmem_limit_bytes=MEMORY)
    weight = 20 if side == 1 else 0
    cost = pl.CostEstimate(flops=weight * total_rows * width * depth, bytes_accessed=0, transcendentals=0)
    options = dict(grid=(depth // tile,), compiler_params=params, cost_estimate=cost)
    return specs, operands, options, tile, depth


def down_first(hidden, pieces, blocks):
    specs, operands, options, tile, depth = down_operands(hidden, pieces, 1)
    rows = hidden.shape[0] // CORES
    return pl.pallas_call(
        functools.partial(down_kernel, len(pieces)),
        in_specs=specs,
        out_specs=[pl.BlockSpec((rows, tile), lambda i: (0, i))] * len(pieces),
        out_shape=[jax.ShapeDtypeStruct((rows, depth), jnp.bfloat16)] * len(pieces),
        **options,
    )(*operands)


def down_second(hidden, pieces, blocks, arrived):
    specs, operands, options, tile, depth = down_operands(hidden, pieces, 0)
    shape = (blocks // 4, hidden.shape[0] // blocks, depth * len(pieces))
    half = hidden.shape[0] // CORES
    return pl.pallas_call(
        functools.partial(down_add_kernel, len(pieces), tile),
        in_specs=specs + [pl.BlockSpec((half, tile), lambda i: (0, i))] * len(pieces),
        out_specs=[whole(*shape)] * 2,
        out_shape=[
            jax.ShapeDtypeStruct(shape, jnp.float32),
            jax.ShapeDtypeStruct(shape, jnp.bfloat16),
        ],
        scratch_shapes=[pltpu.VMEM((half, tile), jnp.float32)],
        **options,
    )(*operands, *arrived)


def down_and_return(hidden, pieces, blocks):
    arrived = [flip(part, "ctx", 1) for part in down_first(hidden, pieces, blocks)]
    kept, sent = down_second(hidden, pieces, blocks, arrived)
    first_sent = sent
    bit = 2
    while True:
        home = flip(sent, "ctx", bit)
        if kept.shape[0] == 1:
            return kept[0], home[0], first_sent
        total = kept + home.astype(jnp.float32)
        total = total.reshape(total.shape[0] // 2, 2, *total.shape[1:])
        kept, sent = total[:, 0], total[:, 1].astype(jnp.bfloat16)
        bit *= 2


def per_device(
    inputs,
    queries,
    kv_down,
    latent_gain,
    kv_up,
    out_proj,
    post_gain,
    expert_ids,
    gates,
    gate_up,
    down_proj,
):
    tokens = inputs[0]
    rows, width_model = tokens.shape
    ctx_size = lax.axis_size("ctx")
    rank = lax.axis_index("ctx")
    here = lax.axis_index("fsdp")
    local_experts = gate_up.shape[0]
    experts = local_experts * ctx_size

    up_pieces = first_step(gate_up)

    row_iota = jnp.arange(rows, dtype=jnp.int32)
    positions = rank * rows + row_iota
    cosine, sine = swing_tables(positions)
    cache = compress(
        tokens, kv_down, latent_gain, cosine, sine, pick_major(expert_ids), pick_major(gates), experts
    )
    bits = ctx_bits()
    held = spread({0: cache}, bits[:-1])
    owners = jnp.bitwise_xor(rank, jnp.arange(ctx_size, dtype=jnp.int32))
    key_pos = (owners[:, None] * rows + row_iota[None, :]).reshape(1, -1)
    row_pos = positions[:, None]
    post_gain = post_gain[None, :]
    held = {o: after(block, key_pos, row_pos, post_gain) if o else block for o, block in held.items()}
    held = spread(held, bits[-1:])
    keys = [held[o] for o in range(ctx_size)]
    attn_out, routed = attend(
        queries[0],
        kv_up,
        keys,
        key_pos,
        row_pos,
        cosine,
        sine,
        out_proj,
        tokens,
        post_gain,
    )

    held = spread({0: routed}, bits[:1])
    up_pieces = {o: [after(p[0], held[bits[0]])] for o, p in up_pieces.items()}
    up_far, up_halves = second_step(up_pieces)
    held = {o: after(block, *up_halves) for o, block in held.items()} if up_halves else held
    held = spread(held, bits[1:])
    gathered = [held[o] for o in range(ctx_size)]
    last_up = [p for o in sorted(up_far) for p in up_far[o]]
    down_pieces = first_step(after(down_proj, *last_up, *gathered))
    index = jnp.stack([here, rank * local_experts]).astype(jnp.int32)
    up_pieces = {**up_pieces, **up_far}
    hidden = up(index, gathered, keys, experts, up_pieces)
    depth = down_proj.shape[1]
    moe = jnp.zeros((rows, width_model), jnp.bfloat16)
    groups = [(0,), (1, 2), None]
    returned = []
    earlier = []
    for offsets in groups:
        if offsets is None:
            offsets = tuple(sorted(down_far))
        held = after(hidden, *earlier) if earlier else hidden
        pieces = [down_pieces[offset] for offset in offsets]
        own, home, sent = down_and_return(held, pieces, ctx_size)
        earlier = [sent]
        if offsets == (1, 2):
            earlier = [earlier[0], returned[0][2]]
        returned.append((offsets, own, home))
        if offsets == (0,):
            down_pieces = {o: [after(p[0], *earlier)] for o, p in down_pieces.items()}
            down_far, down_halves = second_step(down_pieces)
            down_pieces.update(down_far)
            earlier = [*earlier, *down_halves]
    for offsets, own, home in returned:
        if offsets == (1, 2):
            home = after(home, *earlier)
        own += home.astype(jnp.float32)
        owned = own.astype(jnp.bfloat16)
        for part, offset in enumerate(offsets):
            columns = owned[:, part * depth : (part + 1) * depth]
            start = jnp.bitwise_xor(here, offset) * depth
            moe = lax.dynamic_update_slice(moe, columns, (0, start))
    return (attn_out[None], moe[None])


def solution(mesh):
    in_specs = (
        P("fsdp", "ctx", None),
        P("fsdp", "ctx", None),
        P(),
        P(),
        P(),
        P(),
        P(),
        P("fsdp", "ctx", None),
        P("fsdp", "ctx", None),
        P("ctx", "fsdp", None),
        P("ctx", "fsdp", None),
    )
    out_specs = (P("fsdp", "ctx", None), P("fsdp", "ctx", None))
    return jax.shard_map(
        per_device, mesh=mesh, in_specs=in_specs, out_specs=out_specs, check_vma=False
    )
```

```python
import functools
import math

import jax
import jax.numpy as jnp
from jax import lax
from jax.experimental import pallas as pl
from jax.experimental.pallas import tpu as pltpu
from jax.sharding import PartitionSpec as P

HEADS = 16
NOPE = 128
ROPE = 64
VDIM = 128
LANES = 128

EPSILON = 1e-06
NEG_LARGE = -1e30
CORES = 2
NT = (((1,), (1,)), ((), ()))
MEMORY = 56 * 2**20
CHUNK = 512


def dot(left, right):
    return jnp.dot(left, right, preferred_element_type=jnp.float32)


def dot_nt(left, right):
    return lax.dot_general(left, right, NT, preferred_element_type=jnp.float32)


def free():
    return pl.CostEstimate(flops=0, bytes_accessed=0, transcendentals=0)


def normalize(values, gain):
    mean_sq = jnp.mean(values * values, axis=-1, keepdims=True)
    return values * lax.rsqrt(mean_sq + EPSILON) * gain


def swing_tables(positions):
    half = ROPE // 2
    lane = jnp.arange(LANES, dtype=jnp.int32)
    turn_of = (lane % half).astype(jnp.float32)
    freqs = jnp.exp(-(2.0 * turn_of / ROPE) * math.log(10000.0))
    angles = positions.astype(jnp.float32)[:, None] * freqs[None, :]
    cosine = jnp.where(lane < ROPE, jnp.cos(angles), 0.0)
    sine = jnp.where(lane < half, -jnp.sin(angles), jnp.where(lane < ROPE, jnp.sin(angles), 0.0))
    return cosine, sine


def swing(values, cosine, sine):
    half = ROPE // 2
    lane = lax.broadcasted_iota(jnp.int32, values.shape, 1)
    swapped = jnp.where(
        lane < half, pltpu.roll(values, LANES - half, 1), pltpu.roll(values, half, 1)
    )
    return values * cosine + swapped * sine


def flip(values, axis, mask):
    size = lax.axis_size(axis)
    return lax.ppermute(values, axis, [(i, i ^ mask) for i in range(size)])


def spread(held, bits):
    held = dict(held)
    for bit in bits:
        held.update({o | bit: flip(block, "ctx", bit) for o, block in list(held.items())})
    return held


def ctx_bits():
    size = lax.axis_size("ctx")
    return [1 << b for b in reversed(range(size.bit_length() - 1))]


def after(value, *earlier):
    return lax.optimization_barrier((value, *earlier))[0]


def first_step(shard):
    return {0: [shard], 1: [flip(shard, "fsdp", 1)], 2: [flip(shard, "fsdp", 2)]}


def second_step(pieces):
    size = lax.axis_size("fsdp")
    half = pieces[0][0].shape[0] // 2
    if size == 4:
        low_half, high_half = pieces[1][0][:half], pieces[2][0][half:]
        low = flip(low_half, "fsdp", 2)
        high = flip(high_half, "fsdp", 1)
        return {3: [low, high]}, [low_half, high_half]
    more = {3: [flip(pieces[1][0], "fsdp", 2)]}
    held = {**pieces, **more}
    bit = 4
    while bit < size:
        new = {o | bit: [flip(p[0], "fsdp", bit)] for o, p in held.items()}
        more.update(new)
        held.update(new)
        bit *= 2
    return more, []


def pick_major(values):
    return jnp.transpose(values, (2, 0, 1))


def compress_kernel(
    experts, token_ref, kv_ref, gain_ref, cos_ref, sin_ref, ids_ref, gates_ref, out_ref, pad_ref
):
    width = gain_ref.shape[0]
    compressed = dot_nt(token_ref[...], kv_ref[...])
    latent = normalize(compressed[:, :width], gain_ref[...].astype(jnp.float32)[None, :])
    out_ref[:, :width] = latent.astype(jnp.bfloat16)
    pad_ref[...] = jnp.zeros_like(pad_ref)
    pad_ref[:, :ROPE] = compressed[:, width:]
    swung = swing(pad_ref[...], cos_ref[...], sin_ref[...])
    lane = lax.broadcasted_iota(jnp.int32, swung.shape, 1)
    line = lax.broadcasted_iota(jnp.int32, swung.shape[::-1], 0)
    table = jnp.zeros(line.shape, jnp.float32)
    for k in range(ids_ref.shape[0]):
        pick = ids_ref[k] + ROPE
        named = (pick == line) | (pick + experts == line)
        table += jnp.where(named, gates_ref[k], 0.0)
    table = table.T
    high = table.astype(jnp.bfloat16).astype(jnp.float32)
    table = jnp.where(lane < ROPE + experts, high, table - high)
    out_ref[:, width:] = jnp.where(lane < ROPE, swung, table).astype(jnp.bfloat16)


def compress(tokens, kv_down, latent_gain, cosine, sine, ids, gates, experts):
    rows = tokens.shape[0]
    return pl.pallas_call(
        functools.partial(compress_kernel, experts),
        out_shape=jax.ShapeDtypeStruct((rows, latent_gain.shape[0] + LANES), jnp.bfloat16),
        scratch_shapes=[pltpu.VMEM((rows, LANES), jnp.float32)],
        compiler_params=pltpu.CompilerParams(vmem_limit_bytes=MEMORY),
        cost_estimate=free(),
    )(tokens, kv_down.T, latent_gain, cosine, sine, ids, gates)


def attend_kernel(
    pairs,
    blocks,
    query_ref,
    up_ref,
    key_pos_ref,
    row_pos_ref,
    cos_ref,
    sin_ref,
    out_proj_ref,
    token_ref,
    gain_ref,
    *refs,
):
    key_refs = refs[:blocks]
    attn_ref, routed_ref, acc_ref, packed_ref, bias_ref, keys_ref, turned_ref = refs[blocks:]
    rows = token_ref.shape[0]
    latent_width = up_ref.shape[0]
    head_width = NOPE + VDIM
    scale = (NOPE + ROPE) ** (-0.5)
    step = pl.program_id(0)

    @pl.when(step == 0)
    def _():
        acc_ref[...] = jnp.zeros_like(acc_ref)
        bias_ref[...] = jnp.where(key_pos_ref[...] <= row_pos_ref[...], 0.0, NEG_LARGE)
        for i, ref in enumerate(key_refs):
            keys_ref[i * rows : (i + 1) * rows, :] = ref[...]
            turned_ref[:, i * rows : (i + 1) * rows] = ref[...].T

    cosine, sine = cos_ref[...], sin_ref[...]
    lane = lax.broadcasted_iota(jnp.int32, (rows, LANES), 1)
    for pair in range(pairs):
        base = pair * 2 * (NOPE + ROPE)
        middle = query_ref[:, base + LANES : base + 2 * LANES].astype(jnp.float32)
        last = query_ref[:, base + 2 * LANES : base + 3 * LANES].astype(jnp.float32)
        middle_back, last_back = pltpu.roll(middle, ROPE, 1), pltpu.roll(last, ROPE, 1)
        plain = (
            query_ref[:, base : base + LANES],
            jnp.where(lane < ROPE, middle_back, last_back).astype(jnp.bfloat16),
        )
        turned = (middle, last_back)
        for h in range(2):
            at = (pair * 2 + h) * head_width
            here = slice((pair * 2 + h) * rows, (pair * 2 + h + 1) * rows)
            absorbed = dot_nt(plain[h], up_ref[:, at : at + NOPE])
            packed_ref[here, :latent_width] = (absorbed * scale).astype(jnp.bfloat16)
            swung = swing(turned[h], cosine, sine)
            packed_ref[here, latent_width:] = (swung * scale).astype(jnp.bfloat16)
        packed = packed_ref[pair * 2 * rows : (pair + 1) * 2 * rows, :]
        scores = dot(packed, turned_ref[...])
        bias = bias_ref[...]
        scores = scores + jnp.concatenate([bias, bias], axis=0)
        expo = jnp.exp(scores - jnp.max(scores, axis=1, keepdims=True))
        total = jnp.sum(expo, axis=1, keepdims=True)
        context = dot(expo.astype(jnp.bfloat16), keys_ref[:, :latent_width])
        context = (context / total).astype(jnp.bfloat16)
        heads = []
        for h in range(2):
            at = (pair * 2 + h) * head_width + NOPE
            heads.append(dot(context[h * rows : (h + 1) * rows], up_ref[:, at : at + VDIM]))
        heads = jnp.concatenate(heads, axis=1).astype(jnp.bfloat16)
        acc_ref[...] += dot(heads, out_proj_ref[pair * 2 * VDIM : (pair + 1) * 2 * VDIM, :])

    @pl.when(step == pl.num_programs(0) - 1)
    def _():
        attn = acc_ref[...]
        attn_ref[...] = attn.astype(jnp.bfloat16)
        routed = normalize(
            token_ref[...].astype(jnp.float32) + attn, gain_ref[...].astype(jnp.float32)
        )
        routed_ref[...] = routed.astype(jnp.bfloat16)


def attend(queries, kv_up, keys, key_pos, row_pos, cosine, sine, out_proj, tokens, post_gain):
    rows, width_model = tokens.shape
    pairs = 2
    steps = HEADS // (2 * pairs)
    latent_width = kv_up.shape[0]
    key_width = keys[0].shape[1]
    count = key_pos.shape[1]

    def whole(*shape):
        return pl.BlockSpec(shape, lambda i: (0, 0))

    return pl.pallas_call(
        functools.partial(attend_kernel, pairs, len(keys)),
        grid=(steps,),
        in_specs=[
            pl.BlockSpec((rows, pairs * 2 * (NOPE + ROPE)), lambda i: (0, i)),
            pl.BlockSpec((latent_width, pairs * 2 * (NOPE + VDIM)), lambda i: (0, i)),
            whole(1, count),
            whole(rows, 1),
            whole(rows, LANES),
            whole(rows, LANES),
            pl.BlockSpec((pairs * 2 * VDIM, width_model), lambda i: (i, 0)),
            whole(rows, width_model),
            whole(1, width_model),
        ]
        + [whole(rows, key_width)] * len(keys),
        out_specs=[whole(rows, width_model)] * 2,
        out_shape=[jax.ShapeDtypeStruct((rows, width_model), jnp.bfloat16)] * 2,
        scratch_shapes=[
            pltpu.VMEM((rows, width_model), jnp.float32),
            pltpu.VMEM((pairs * 2 * rows, key_width), jnp.bfloat16),
            pltpu.VMEM((rows, count), jnp.float32),
            pltpu.VMEM((count, key_width), jnp.bfloat16),
            pltpu.VMEM((key_width, count), jnp.bfloat16),
        ],
        compiler_params=pltpu.CompilerParams(vmem_limit_bytes=MEMORY),
        cost_estimate=free(),
    )(
        queries,
        kv_up,
        key_pos,
        row_pos,
        cosine,
        sine,
        out_proj,
        tokens,
        post_gain,
        *keys,
    )


def up_kernel(layout, depth, experts, blocks, index_ref, *refs):
    x_refs, table_refs = refs[:blocks], refs[blocks : 2 * blocks]
    weights = refs[2 * blocks : -4]
    out_ref, x_ref, factor_ref, w_ref = refs[-4:]
    expert = pl.program_id(0)
    me = index_ref[0]
    named = index_ref[1] + expert + ROPE
    rows = x_refs[0].shape[0]
    tile = out_ref.shape[1]

    @pl.when((expert == 0) & (pl.program_id(1) == 0))
    def _():
        for i in range(blocks):
            place = (i % CORES) * (blocks // CORES) + i // CORES
            here = slice(place * rows, (place + 1) * rows)
            for part, (offset, _, _) in enumerate(layout):
                at = pl.ds(pl.multiple_of(jnp.bitwise_xor(me, offset) * depth, depth), depth)
                x_ref[here, part * depth : (part + 1) * depth] = x_refs[i][:, at]

    @pl.when(pl.program_id(1) == 0)
    def _():
        for i in range(blocks):
            place = (i % CORES) * (blocks // CORES) + i // CORES
            here = slice(place * rows, (place + 1) * rows)
            table = table_refs[i][...].astype(jnp.float32)
            lane = lax.broadcasted_iota(jnp.int32, table.shape, 1)
            mine = (lane == named) | (lane == named + experts)
            factor_ref[here, :] = jnp.sum(jnp.where(mine, table, 0.0), axis=1, keepdims=True)

    for part, (_, first, per) in enumerate(layout):
        here = slice(part * depth, (part + 1) * depth)

        def fill(at, here=here):
            w_ref[here, :tile] = weights[2 * at][0]
            w_ref[here, tile:] = weights[2 * at + 1][0]

        if per > 1:
            fill(first)
        else:
            pl.when(expert == 0)(functools.partial(fill, first))
            pl.when(expert == 1)(functools.partial(fill, first + 1))
    step = min(CHUNK, blocks * rows)
    for start in range(0, blocks * rows, step):
        here = slice(start, start + step)
        joint = dot(x_ref[here, :], w_ref[...])
        gate_sum, up_sum = joint[:, :tile], joint[:, tile:]
        hidden = gate_sum / (1.0 + jnp.exp(-gate_sum)) * up_sum * factor_ref[here, :]
        out_ref[here, :] = hidden.astype(jnp.bfloat16)


def up(index, tokens, tables, experts, pieces):
    rows, width_model = tokens[0].shape
    blocks = len(tokens)
    depth, joint_width = pieces[0][0].shape[1:]
    width = joint_width // 2
    tile = 256
    tiles = width // tile
    layout, operands, specs = [], [], []
    for offset in sorted(pieces):
        parts = pieces[offset]
        per = parts[0].shape[0]
        layout.append((offset, len(operands) // 2, per))
        for number, part in enumerate(parts):
            for side in range(2):

                def place(e, j, s, per=per, number=number, side=side):
                    if per > 1:
                        return e, 0, j + side * tiles
                    still = tiles - 1 if number == 0 else 0
                    return 0, 0, jnp.where(e == number, j, still) + side * tiles

                operands.append(part)
                specs.append(pl.BlockSpec((1, depth, tile), place))
    last = tables[0].shape[1] // LANES - 1
    return pl.pallas_call(
        functools.partial(up_kernel, layout, depth, experts, blocks),
        grid_spec=pltpu.PrefetchScalarGridSpec(
            num_scalar_prefetch=1,
            grid=(2, tiles),
            in_specs=[pl.BlockSpec((rows, width_model), lambda e, j, s: (0, 0))] * blocks
            + [pl.BlockSpec((rows, LANES), lambda e, j, s: (0, last))] * blocks
            + specs,
            out_specs=pl.BlockSpec((blocks * rows, tile), lambda e, j, s: (0, e * tiles + j)),
            scratch_shapes=[
                pltpu.VMEM((blocks * rows, width_model), jnp.bfloat16),
                pltpu.VMEM((blocks * rows, 1), jnp.float32),
                pltpu.VMEM((width_model, 2 * tile), jnp.bfloat16),
            ],
        ),
        out_shape=jax.ShapeDtypeStruct((blocks * rows, 2 * width), jnp.bfloat16),
        compiler_params=pltpu.CompilerParams(vmem_limit_bytes=MEMORY),
        cost_estimate=free(),
    )(index, *tokens, *tables, *operands)


def product(hidden, weights, part):
    first, second = weights[2 * part], weights[2 * part + 1]
    width = first.shape[2]
    return dot_nt(hidden[:, :width], first[0]) + dot_nt(hidden[:, width:], second[0])


def down_kernel(parts, *refs):
    hidden, weights, out_refs = refs[0], refs[1 : 1 + 2 * parts], refs[1 + 2 * parts :]
    for part in range(parts):
        out_refs[part][...] = product(hidden, weights, part).astype(jnp.bfloat16)


def down_add_kernel(parts, tile, *refs):
    hidden, weights, arrived = refs[0], refs[1 : 1 + 2 * parts], refs[1 + 2 * parts : 1 + 3 * parts]
    kept_ref, sent_ref, sum_ref = refs[1 + 3 * parts :]
    count, rows, columns = kept_ref.shape
    depth = columns // parts
    for part in range(parts):
        at = pl.ds(pl.multiple_of(part * depth + pl.program_id(0) * tile, tile), tile)
        sum_ref[...] = product(hidden, weights, part) + arrived[part][...].astype(jnp.float32)
        for i in range(count):
            kept_ref[i, :, at] = sum_ref[2 * i * rows : (2 * i + 1) * rows, :]
            sent = sum_ref[(2 * i + 1) * rows : (2 * i + 2) * rows, :]
            sent_ref[i, :, at] = sent.astype(jnp.bfloat16)


def whole(*shape):
    return pl.BlockSpec(shape, lambda *i: (0,) * len(shape))


def down_operands(hidden, pieces, side):
    total_rows = hidden.shape[0]
    depth, width = pieces[0][0].shape[1:]
    tile = min(256, depth)
    specs = [pl.BlockSpec((total_rows // CORES, hidden.shape[1]), lambda i: (side, 0))]
    operands = [hidden]
    for parts in pieces:
        per = parts[0].shape[0]
        for expert in range(2):
            specs.append(
                pl.BlockSpec((1, tile, width), lambda i, at=expert % per: (at, i, 0))
            )
            operands.append(parts[expert // per])
    params = pltpu.CompilerParams(vmem_limit_bytes=MEMORY)
    weight = 20 if side == 1 else 0
    cost = pl.CostEstimate(flops=weight * total_rows * width * depth, bytes_accessed=0, transcendentals=0)
    options = dict(grid=(depth // tile,), compiler_params=params, cost_estimate=cost)
    return specs, operands, options, tile, depth


def down_first(hidden, pieces, blocks):
    specs, operands, options, tile, depth = down_operands(hidden, pieces, 1)
    rows = hidden.shape[0] // CORES
    return pl.pallas_call(
        functools.partial(down_kernel, len(pieces)),
        in_specs=specs,
        out_specs=[pl.BlockSpec((rows, tile), lambda i: (0, i))] * len(pieces),
        out_shape=[jax.ShapeDtypeStruct((rows, depth), jnp.bfloat16)] * len(pieces),
        **options,
    )(*operands)


def down_second(hidden, pieces, blocks, arrived):
    specs, operands, options, tile, depth = down_operands(hidden, pieces, 0)
    shape = (blocks // 4, hidden.shape[0] // blocks, depth * len(pieces))
    half = hidden.shape[0] // CORES
    return pl.pallas_call(
        functools.partial(down_add_kernel, len(pieces), tile),
        in_specs=specs + [pl.BlockSpec((half, tile), lambda i: (0, i))] * len(pieces),
        out_specs=[whole(*shape)] * 2,
        out_shape=[
            jax.ShapeDtypeStruct(shape, jnp.float32),
            jax.ShapeDtypeStruct(shape, jnp.bfloat16),
        ],
        scratch_shapes=[pltpu.VMEM((half, tile), jnp.float32)],
        **options,
    )(*operands, *arrived)


def down_and_send(hidden, pieces, blocks):
    arrived = [flip(part, "ctx", 1) for part in down_first(hidden, pieces, blocks)]
    kept, sent = down_second(hidden, pieces, blocks, arrived)
    return kept, flip(sent, "ctx", 2), sent


def send_home(kept, home):
    bit, sent = 2, home
    while kept.shape[0] > 1:
        bit *= 2
        total = kept + home.astype(jnp.float32)
        total = total.reshape(total.shape[0] // 2, 2, *total.shape[1:])
        kept, sent = total[:, 0], total[:, 1].astype(jnp.bfloat16)
        home = flip(sent, "ctx", bit)
    return kept[0], home[0], sent


def per_device(
    inputs,
    queries,
    kv_down,
    latent_gain,
    kv_up,
    out_proj,
    post_gain,
    expert_ids,
    gates,
    gate_up,
    down_proj,
):
    tokens = inputs[0]
    rows, width_model = tokens.shape
    ctx_size = lax.axis_size("ctx")
    rank = lax.axis_index("ctx")
    here = lax.axis_index("fsdp")
    local_experts = gate_up.shape[0]
    experts = local_experts * ctx_size

    up_pieces = first_step(gate_up)

    row_iota = jnp.arange(rows, dtype=jnp.int32)
    positions = rank * rows + row_iota
    cosine, sine = swing_tables(positions)
    cache = compress(
        tokens, kv_down, latent_gain, cosine, sine, pick_major(expert_ids), pick_major(gates), experts
    )
    bits = ctx_bits()
    held = spread({0: cache}, bits[:-1])
    owners = jnp.bitwise_xor(rank, jnp.arange(ctx_size, dtype=jnp.int32))
    key_pos = (owners[:, None] * rows + row_iota[None, :]).reshape(1, -1)
    row_pos = positions[:, None]
    post_gain = post_gain[None, :]
    held = {o: after(block, key_pos, row_pos, post_gain) if o else block for o, block in held.items()}
    held = spread(held, bits[-1:])
    keys = [held[o] for o in range(ctx_size)]
    attn_out, routed = attend(
        queries[0],
        kv_up,
        keys,
        key_pos,
        row_pos,
        cosine,
        sine,
        out_proj,
        tokens,
        post_gain,
    )

    held = spread({0: routed}, bits[:1])
    up_pieces = {o: [after(p[0], held[bits[0]])] for o, p in up_pieces.items()}
    up_far, up_halves = second_step(up_pieces)
    held = {o: after(block, *up_halves) for o, block in held.items()} if up_halves else held
    held = spread(held, bits[1:])
    gathered = [held[o] for o in range(ctx_size)]
    last_up = [p for o in sorted(up_far) for p in up_far[o]]
    down_pieces = first_step(after(down_proj, *last_up, *gathered))
    index = jnp.stack([here, rank * local_experts]).astype(jnp.int32)
    up_pieces = {**up_pieces, **up_far}
    hidden = up(index, gathered, keys, experts, up_pieces)
    depth = down_proj.shape[1]
    moe = jnp.zeros((rows, width_model), jnp.bfloat16)
    groups = [(0,), (1, 2), None]
    returned = {}
    earlier = []
    for offsets in groups:
        if offsets is None:
            offsets = tuple(sorted(down_far))
        held = after(hidden, *earlier) if earlier else hidden
        pieces = [down_pieces[offset] for offset in offsets]
        kept, home, sent = down_and_send(held, pieces, ctx_size)
        earlier = [sent]
        if offsets == (0,):
            returned[offsets] = send_home(kept, home)
        elif offsets == (1, 2):
            near_sums = (kept, home)
            earlier = [sent, returned[(0,)][1]]
        else:
            near_kept, near_home = near_sums
            returned[(1, 2)] = send_home(near_kept, after(near_home, sent))
            returned[offsets] = send_home(kept, home)
        if offsets == (0,):
            down_pieces = {o: [after(p[0], *earlier)] for o, p in down_pieces.items()}
            down_far, down_halves = second_step(down_pieces)
            down_pieces.update(down_far)
            earlier = [*earlier, *down_halves]
    for offsets, (own, home, _) in returned.items():
        if offsets == (1, 2):
            home = after(home, returned[tuple(sorted(down_far))][2])
        own += home.astype(jnp.float32)
        owned = own.astype(jnp.bfloat16)
        for part, offset in enumerate(offsets):
            columns = owned[:, part * depth : (part + 1) * depth]
            start = jnp.bitwise_xor(here, offset) * depth
            moe = lax.dynamic_update_slice(moe, columns, (0, start))
    return (attn_out[None], moe[None])


def solution(mesh):
    in_specs = (
        P("fsdp", "ctx", None),
        P("fsdp", "ctx", None),
        P(),
        P(),
        P(),
        P(),
        P(),
        P("fsdp", "ctx", None),
        P("fsdp", "ctx", None),
        P("ctx", "fsdp", None),
        P("ctx", "fsdp", None),
    )
    out_specs = (P("fsdp", "ctx", None), P("fsdp", "ctx", None))
    return jax.shard_map(
        per_device, mesh=mesh, in_specs=in_specs, out_specs=out_specs, check_vma=False
    )
```

```python
import functools
import math

import jax
import jax.numpy as jnp
from jax import lax
from jax.experimental import pallas as pl
from jax.experimental.pallas import tpu as pltpu
from jax.sharding import PartitionSpec as P

HEADS = 16
NOPE = 128
ROPE = 64
VDIM = 128
LANES = 128

EPSILON = 1e-06
NEG_LARGE = -1e30
CORES = 2
NT = (((1,), (1,)), ((), ()))
MEMORY = 56 * 2**20
CHUNK = 512


def dot(left, right):
    return jnp.dot(left, right, preferred_element_type=jnp.float32)


def dot_nt(left, right):
    return lax.dot_general(left, right, NT, preferred_element_type=jnp.float32)


def free():
    return pl.CostEstimate(flops=0, bytes_accessed=0, transcendentals=0)


def normalize(values, gain):
    mean_sq = jnp.mean(values * values, axis=-1, keepdims=True)
    return values * lax.rsqrt(mean_sq + EPSILON) * gain


def swing_tables(positions):
    half = ROPE // 2
    lane = jnp.arange(LANES, dtype=jnp.int32)
    turn_of = (lane % half).astype(jnp.float32)
    freqs = jnp.exp(-(2.0 * turn_of / ROPE) * math.log(10000.0))
    angles = positions.astype(jnp.float32)[:, None] * freqs[None, :]
    cosine = jnp.where(lane < ROPE, jnp.cos(angles), 0.0)
    sine = jnp.where(lane < half, -jnp.sin(angles), jnp.where(lane < ROPE, jnp.sin(angles), 0.0))
    return cosine, sine


def swing(values, cosine, sine):
    half = ROPE // 2
    lane = lax.broadcasted_iota(jnp.int32, values.shape, 1)
    swapped = jnp.where(
        lane < half, pltpu.roll(values, LANES - half, 1), pltpu.roll(values, half, 1)
    )
    return values * cosine + swapped * sine


def flip(values, axis, mask):
    size = lax.axis_size(axis)
    return lax.ppermute(values, axis, [(i, i ^ mask) for i in range(size)])


def spread(held, bits):
    held = dict(held)
    for bit in bits:
        held.update({o | bit: flip(block, "ctx", bit) for o, block in list(held.items())})
    return held


def ctx_bits():
    size = lax.axis_size("ctx")
    return [1 << b for b in reversed(range(size.bit_length() - 1))]


def after(value, *earlier):
    return lax.optimization_barrier((value, *earlier))[0]


def first_step(shard):
    return {0: [shard], 1: [flip(shard, "fsdp", 1)], 2: [flip(shard, "fsdp", 2)]}


def second_step(pieces):
    size = lax.axis_size("fsdp")
    half = pieces[0][0].shape[0] // 2
    if size == 4:
        low_half, high_half = pieces[1][0][:half], pieces[2][0][half:]
        low = flip(low_half, "fsdp", 2)
        high = flip(high_half, "fsdp", 1)
        return {3: [low, high]}, [low_half, high_half]
    more = {3: [flip(pieces[1][0], "fsdp", 2)]}
    held = {**pieces, **more}
    bit = 4
    while bit < size:
        new = {o | bit: [flip(p[0], "fsdp", bit)] for o, p in held.items()}
        more.update(new)
        held.update(new)
        bit *= 2
    return more, []


def pick_major(values):
    return jnp.transpose(values, (2, 0, 1))


def compress_kernel(
    experts, token_ref, kv_ref, gain_ref, cos_ref, sin_ref, ids_ref, gates_ref, out_ref, pad_ref
):
    width = gain_ref.shape[0]
    compressed = dot_nt(token_ref[...], kv_ref[...])
    latent = normalize(compressed[:, :width], gain_ref[...].astype(jnp.float32)[None, :])
    out_ref[:, :width] = latent.astype(jnp.bfloat16)
    pad_ref[...] = jnp.zeros_like(pad_ref)
    pad_ref[:, :ROPE] = compressed[:, width:]
    swung = swing(pad_ref[...], cos_ref[...], sin_ref[...])
    lane = lax.broadcasted_iota(jnp.int32, swung.shape, 1)
    line = lax.broadcasted_iota(jnp.int32, swung.shape[::-1], 0)
    table = jnp.zeros(line.shape, jnp.float32)
    for k in range(ids_ref.shape[0]):
        pick = ids_ref[k] + ROPE
        named = (pick == line) | (pick + experts == line)
        table += jnp.where(named, gates_ref[k], 0.0)
    table = table.T
    high = table.astype(jnp.bfloat16).astype(jnp.float32)
    table = jnp.where(lane < ROPE + experts, high, table - high)
    out_ref[:, width:] = jnp.where(lane < ROPE, swung, table).astype(jnp.bfloat16)


def compress(tokens, kv_down, latent_gain, cosine, sine, ids, gates, experts):
    rows = tokens.shape[0]
    return pl.pallas_call(
        functools.partial(compress_kernel, experts),
        out_shape=jax.ShapeDtypeStruct((rows, latent_gain.shape[0] + LANES), jnp.bfloat16),
        scratch_shapes=[pltpu.VMEM((rows, LANES), jnp.float32)],
        compiler_params=pltpu.CompilerParams(vmem_limit_bytes=MEMORY),
        cost_estimate=free(),
    )(tokens, kv_down.T, latent_gain, cosine, sine, ids, gates)


def attend_kernel(
    pairs,
    blocks,
    query_ref,
    up_ref,
    key_pos_ref,
    row_pos_ref,
    cos_ref,
    sin_ref,
    out_proj_ref,
    token_ref,
    gain_ref,
    *refs,
):
    key_refs = refs[:blocks]
    attn_ref, routed_ref, acc_ref, packed_ref, bias_ref, keys_ref, turned_ref = refs[blocks:]
    rows = token_ref.shape[0]
    latent_width = up_ref.shape[0]
    head_width = NOPE + VDIM
    scale = (NOPE + ROPE) ** (-0.5)
    step = pl.program_id(0)

    @pl.when(step == 0)
    def _():
        acc_ref[...] = jnp.zeros_like(acc_ref)
        bias_ref[...] = jnp.where(key_pos_ref[...] <= row_pos_ref[...], 0.0, NEG_LARGE)
        for i, ref in enumerate(key_refs):
            keys_ref[i * rows : (i + 1) * rows, :] = ref[...]
            turned_ref[:, i * rows : (i + 1) * rows] = ref[...].T

    cosine, sine = cos_ref[...], sin_ref[...]
    lane = lax.broadcasted_iota(jnp.int32, (rows, LANES), 1)
    for pair in range(pairs):
        base = pair * 2 * (NOPE + ROPE)
        middle = query_ref[:, base + LANES : base + 2 * LANES].astype(jnp.float32)
        last = query_ref[:, base + 2 * LANES : base + 3 * LANES].astype(jnp.float32)
        middle_back, last_back = pltpu.roll(middle, ROPE, 1), pltpu.roll(last, ROPE, 1)
        plain = (
            query_ref[:, base : base + LANES],
            jnp.where(lane < ROPE, middle_back, last_back).astype(jnp.bfloat16),
        )
        turned = (middle, last_back)
        for h in range(2):
            at = (pair * 2 + h) * head_width
            here = slice((pair * 2 + h) * rows, (pair * 2 + h + 1) * rows)
            absorbed = dot_nt(plain[h], up_ref[:, at : at + NOPE])
            packed_ref[here, :latent_width] = (absorbed * scale).astype(jnp.bfloat16)
            swung = swing(turned[h], cosine, sine)
            packed_ref[here, latent_width:] = (swung * scale).astype(jnp.bfloat16)
        packed = packed_ref[pair * 2 * rows : (pair + 1) * 2 * rows, :]
        scores = dot(packed, turned_ref[...])
        bias = bias_ref[...]
        scores = scores + jnp.concatenate([bias, bias], axis=0)
        expo = jnp.exp(scores - jnp.max(scores, axis=1, keepdims=True))
        total = jnp.sum(expo, axis=1, keepdims=True)
        context = dot(expo.astype(jnp.bfloat16), keys_ref[:, :latent_width])
        context = (context / total).astype(jnp.bfloat16)
        heads = []
        for h in range(2):
            at = (pair * 2 + h) * head_width + NOPE
            heads.append(dot(context[h * rows : (h + 1) * rows], up_ref[:, at : at + VDIM]))
        heads = jnp.concatenate(heads, axis=1).astype(jnp.bfloat16)
        acc_ref[...] += dot(heads, out_proj_ref[pair * 2 * VDIM : (pair + 1) * 2 * VDIM, :])

    @pl.when(step == pl.num_programs(0) - 1)
    def _():
        attn = acc_ref[...]
        attn_ref[...] = attn.astype(jnp.bfloat16)
        routed = normalize(
            token_ref[...].astype(jnp.float32) + attn, gain_ref[...].astype(jnp.float32)
        )
        routed_ref[...] = routed.astype(jnp.bfloat16)


def attend(queries, kv_up, keys, key_pos, row_pos, cosine, sine, out_proj, tokens, post_gain):
    rows, width_model = tokens.shape
    pairs = 2
    steps = HEADS // (2 * pairs)
    latent_width = kv_up.shape[0]
    key_width = keys[0].shape[1]
    count = key_pos.shape[1]

    def whole(*shape):
        return pl.BlockSpec(shape, lambda i: (0, 0))

    return pl.pallas_call(
        functools.partial(attend_kernel, pairs, len(keys)),
        grid=(steps,),
        in_specs=[
            pl.BlockSpec((rows, pairs * 2 * (NOPE + ROPE)), lambda i: (0, i)),
            pl.BlockSpec((latent_width, pairs * 2 * (NOPE + VDIM)), lambda i: (0, i)),
            whole(1, count),
            whole(rows, 1),
            whole(rows, LANES),
            whole(rows, LANES),
            pl.BlockSpec((pairs * 2 * VDIM, width_model), lambda i: (i, 0)),
            whole(rows, width_model),
            whole(1, width_model),
        ]
        + [whole(rows, key_width)] * len(keys),
        out_specs=[whole(rows, width_model)] * 2,
        out_shape=[jax.ShapeDtypeStruct((rows, width_model), jnp.bfloat16)] * 2,
        scratch_shapes=[
            pltpu.VMEM((rows, width_model), jnp.float32),
            pltpu.VMEM((pairs * 2 * rows, key_width), jnp.bfloat16),
            pltpu.VMEM((rows, count), jnp.float32),
            pltpu.VMEM((count, key_width), jnp.bfloat16),
            pltpu.VMEM((key_width, count), jnp.bfloat16),
        ],
        compiler_params=pltpu.CompilerParams(vmem_limit_bytes=MEMORY),
        cost_estimate=free(),
    )(
        queries,
        kv_up,
        key_pos,
        row_pos,
        cosine,
        sine,
        out_proj,
        tokens,
        post_gain,
        *keys,
    )


def up_kernel(layout, depth, experts, blocks, index_ref, *refs):
    x_refs, table_refs = refs[:blocks], refs[blocks : 2 * blocks]
    weights = refs[2 * blocks : -4]
    out_ref, x_ref, factor_ref, w_ref = refs[-4:]
    expert = pl.program_id(0)
    me = index_ref[0]
    named = index_ref[1] + expert + ROPE
    rows = x_refs[0].shape[0]
    tile = out_ref.shape[1]

    @pl.when((expert == 0) & (pl.program_id(1) == 0))
    def _():
        for i in range(blocks):
            place = (i % CORES) * (blocks // CORES) + i // CORES
            here = slice(place * rows, (place + 1) * rows)
            for part, (offset, _, _) in enumerate(layout):
                at = pl.ds(pl.multiple_of(jnp.bitwise_xor(me, offset) * depth, depth), depth)
                x_ref[here, part * depth : (part + 1) * depth] = x_refs[i][:, at]

    @pl.when(pl.program_id(1) == 0)
    def _():
        for i in range(blocks):
            place = (i % CORES) * (blocks // CORES) + i // CORES
            here = slice(place * rows, (place + 1) * rows)
            table = table_refs[i][...].astype(jnp.float32)
            lane = lax.broadcasted_iota(jnp.int32, table.shape, 1)
            mine = (lane == named) | (lane == named + experts)
            factor_ref[here, :] = jnp.sum(jnp.where(mine, table, 0.0), axis=1, keepdims=True)

    for part, (_, first, per) in enumerate(layout):
        here = slice(part * depth, (part + 1) * depth)

        def fill(at, here=here):
            w_ref[here, :tile] = weights[2 * at][0]
            w_ref[here, tile:] = weights[2 * at + 1][0]

        if per > 1:
            fill(first)
        else:
            pl.when(expert == 0)(functools.partial(fill, first))
            pl.when(expert == 1)(functools.partial(fill, first + 1))
    step = min(CHUNK, blocks * rows)
    for start in range(0, blocks * rows, step):
        here = slice(start, start + step)
        joint = dot(x_ref[here, :], w_ref[...])
        gate_sum, up_sum = joint[:, :tile], joint[:, tile:]
        hidden = gate_sum / (1.0 + jnp.exp(-gate_sum)) * up_sum * factor_ref[here, :]
        out_ref[here, :] = hidden.astype(jnp.bfloat16)


def up(index, tokens, tables, experts, pieces):
    rows, width_model = tokens[0].shape
    blocks = len(tokens)
    depth, joint_width = pieces[0][0].shape[1:]
    width = joint_width // 2
    tile = 256
    tiles = width // tile
    layout, operands, specs = [], [], []
    for offset in sorted(pieces):
        parts = pieces[offset]
        per = parts[0].shape[0]
        layout.append((offset, len(operands) // 2, per))
        for number, part in enumerate(parts):
            for side in range(2):

                def place(e, j, s, per=per, number=number, side=side):
                    if per > 1:
                        return e, 0, j + side * tiles
                    still = tiles - 1 if number == 0 else 0
                    return 0, 0, jnp.where(e == number, j, still) + side * tiles

                operands.append(part)
                specs.append(pl.BlockSpec((1, depth, tile), place))
    last = tables[0].shape[1] // LANES - 1
    return pl.pallas_call(
        functools.partial(up_kernel, layout, depth, experts, blocks),
        grid_spec=pltpu.PrefetchScalarGridSpec(
            num_scalar_prefetch=1,
            grid=(2, tiles),
            in_specs=[pl.BlockSpec((rows, width_model), lambda e, j, s: (0, 0))] * blocks
            + [pl.BlockSpec((rows, LANES), lambda e, j, s: (0, last))] * blocks
            + specs,
            out_specs=pl.BlockSpec((blocks * rows, tile), lambda e, j, s: (0, e * tiles + j)),
            scratch_shapes=[
                pltpu.VMEM((blocks * rows, width_model), jnp.bfloat16),
                pltpu.VMEM((blocks * rows, 1), jnp.float32),
                pltpu.VMEM((width_model, 2 * tile), jnp.bfloat16),
            ],
        ),
        out_shape=jax.ShapeDtypeStruct((blocks * rows, 2 * width), jnp.bfloat16),
        compiler_params=pltpu.CompilerParams(vmem_limit_bytes=MEMORY),
        cost_estimate=free(),
    )(index, *tokens, *tables, *operands)


def product(hidden, weights, part):
    first, second = weights[2 * part], weights[2 * part + 1]
    width = first.shape[2]
    return dot_nt(hidden[:, :width], first[0]) + dot_nt(hidden[:, width:], second[0])


def down_kernel(parts, *refs):
    hidden, weights, out_refs = refs[0], refs[1 : 1 + 2 * parts], refs[1 + 2 * parts :]
    for part in range(parts):
        out_refs[part][...] = product(hidden, weights, part).astype(jnp.bfloat16)


def down_add_kernel(parts, tile, *refs):
    hidden, weights, arrived = refs[0], refs[1 : 1 + 2 * parts], refs[1 + 2 * parts : 1 + 3 * parts]
    kept_ref, sent_ref, sum_ref = refs[1 + 3 * parts :]
    count, rows, columns = kept_ref.shape
    depth = columns // parts
    for part in range(parts):
        at = pl.ds(pl.multiple_of(part * depth + pl.program_id(0) * tile, tile), tile)
        sum_ref[...] = product(hidden, weights, part) + arrived[part][...].astype(jnp.float32)
        for i in range(count):
            kept_ref[i, :, at] = sum_ref[2 * i * rows : (2 * i + 1) * rows, :]
            sent = sum_ref[(2 * i + 1) * rows : (2 * i + 2) * rows, :]
            sent_ref[i, :, at] = sent.astype(jnp.bfloat16)


def whole(*shape):
    return pl.BlockSpec(shape, lambda *i: (0,) * len(shape))


def down_operands(hidden, pieces, side):
    total_rows = hidden.shape[0]
    depth, width = pieces[0][0].shape[1:]
    tile = min(256, depth)
    specs = [pl.BlockSpec((total_rows // CORES, hidden.shape[1]), lambda i: (side, 0))]
    operands = [hidden]
    for parts in pieces:
        per = parts[0].shape[0]
        for expert in range(2):
            specs.append(
                pl.BlockSpec((1, tile, width), lambda i, at=expert % per: (at, i, 0))
            )
            operands.append(parts[expert // per])
    params = pltpu.CompilerParams(vmem_limit_bytes=MEMORY)
    weight = 20 if side == 1 else 0
    cost = pl.CostEstimate(flops=weight * total_rows * width * depth, bytes_accessed=0, transcendentals=0)
    options = dict(grid=(depth // tile,), compiler_params=params, cost_estimate=cost)
    return specs, operands, options, tile, depth


def down_first(hidden, pieces, blocks):
    specs, operands, options, tile, depth = down_operands(hidden, pieces, 1)
    rows = hidden.shape[0] // CORES
    return pl.pallas_call(
        functools.partial(down_kernel, len(pieces)),
        in_specs=specs,
        out_specs=[pl.BlockSpec((rows, tile), lambda i: (0, i))] * len(pieces),
        out_shape=[jax.ShapeDtypeStruct((rows, depth), jnp.bfloat16)] * len(pieces),
        **options,
    )(*operands)


def down_second(hidden, pieces, blocks, arrived):
    specs, operands, options, tile, depth = down_operands(hidden, pieces, 0)
    shape = (blocks // 4, hidden.shape[0] // blocks, depth * len(pieces))
    half = hidden.shape[0] // CORES
    return pl.pallas_call(
        functools.partial(down_add_kernel, len(pieces), tile),
        in_specs=specs + [pl.BlockSpec((half, tile), lambda i: (0, i))] * len(pieces),
        out_specs=[whole(*shape)] * 2,
        out_shape=[
            jax.ShapeDtypeStruct(shape, jnp.float32),
            jax.ShapeDtypeStruct(shape, jnp.bfloat16),
        ],
        scratch_shapes=[pltpu.VMEM((half, tile), jnp.float32)],
        **options,
    )(*operands, *arrived)


def down_and_send(hidden, pieces, blocks):
    arrived = [flip(part, "ctx", 1) for part in down_first(hidden, pieces, blocks)]
    kept, sent = down_second(hidden, pieces, blocks, arrived)
    return kept, flip(sent, "ctx", 2), sent


def send_home(kept, home):
    bit, sent = 2, home
    while kept.shape[0] > 1:
        bit *= 2
        total = kept + home.astype(jnp.float32)
        total = total.reshape(total.shape[0] // 2, 2, *total.shape[1:])
        kept, sent = total[:, 0], total[:, 1].astype(jnp.bfloat16)
        home = flip(sent, "ctx", bit)
    return kept[0], home[0], sent


def per_device(
    inputs,
    queries,
    kv_down,
    latent_gain,
    kv_up,
    out_proj,
    post_gain,
    expert_ids,
    gates,
    gate_up,
    down_proj,
):
    tokens = inputs[0]
    rows, width_model = tokens.shape
    ctx_size = lax.axis_size("ctx")
    rank = lax.axis_index("ctx")
    here = lax.axis_index("fsdp")
    local_experts = gate_up.shape[0]
    experts = local_experts * ctx_size

    up_pieces = first_step(gate_up)

    row_iota = jnp.arange(rows, dtype=jnp.int32)
    positions = rank * rows + row_iota
    cosine, sine = swing_tables(positions)
    cache = compress(
        tokens, kv_down, latent_gain, cosine, sine, pick_major(expert_ids), pick_major(gates), experts
    )
    bits = ctx_bits()
    held = spread({0: cache}, bits[:-1])
    owners = jnp.bitwise_xor(rank, jnp.arange(ctx_size, dtype=jnp.int32))
    key_pos = (owners[:, None] * rows + row_iota[None, :]).reshape(1, -1)
    row_pos = positions[:, None]
    post_gain = post_gain[None, :]
    held = {o: after(block, key_pos, row_pos, post_gain) if o else block for o, block in held.items()}
    held = spread(held, bits[-1:])
    keys = [held[o] for o in range(ctx_size)]
    attn_out, routed = attend(
        queries[0],
        kv_up,
        keys,
        key_pos,
        row_pos,
        cosine,
        sine,
        out_proj,
        tokens,
        post_gain,
    )

    held = spread({0: routed}, bits[:1])
    up_pieces = {o: [after(p[0], held[bits[0]])] for o, p in up_pieces.items()}
    up_far, up_halves = second_step(up_pieces)
    held = {o: after(block, *up_halves) for o, block in held.items()} if up_halves else held
    held = spread(held, bits[1:])
    gathered = [held[o] for o in range(ctx_size)]
    last_up = [p for o in sorted(up_far) for p in up_far[o]]
    down_pieces = first_step(after(down_proj, *last_up, *gathered))
    index = jnp.stack([here, rank * local_experts]).astype(jnp.int32)
    up_pieces = {**up_pieces, **up_far}
    hidden = up(index, gathered, keys, experts, up_pieces)
    depth = down_proj.shape[1]
    moe = jnp.zeros((rows, width_model), jnp.bfloat16)
    groups = [(0,), (1, 2), None]
    returned = {}
    earlier = []
    for offsets in groups:
        if offsets is None:
            offsets = tuple(sorted(down_far))
        held = after(hidden, *earlier) if earlier else hidden
        pieces = [down_pieces[offset] for offset in offsets]
        kept, home, sent = down_and_send(held, pieces, ctx_size)
        earlier = [sent]
        if offsets == (0,):
            returned[offsets] = send_home(kept, home)
        elif offsets == (1, 2):
            near_sums = (kept, home)
        else:
            near_kept, near_home = near_sums
            returned[(1, 2)] = send_home(near_kept, after(near_home, sent))
            returned[offsets] = send_home(kept, home)
        if offsets == (0,):
            down_pieces = {o: [after(p[0], *earlier)] for o, p in down_pieces.items()}
            down_far, down_halves = second_step(down_pieces)
            down_pieces.update(down_far)
            earlier = [*earlier, *down_halves]
    for offsets, (own, home, _) in returned.items():
        if offsets == (1, 2):
            home = after(home, returned[tuple(sorted(down_far))][2])
        if offsets == (0,):
            home = after(home, returned[(1, 2)][2])
        own += home.astype(jnp.float32)
        owned = own.astype(jnp.bfloat16)
        for part, offset in enumerate(offsets):
            columns = owned[:, part * depth : (part + 1) * depth]
            start = jnp.bitwise_xor(here, offset) * depth
            moe = lax.dynamic_update_slice(moe, columns, (0, start))
    return (attn_out[None], moe[None])


def solution(mesh):
    in_specs = (
        P("fsdp", "ctx", None),
        P("fsdp", "ctx", None),
        P(),
        P(),
        P(),
        P(),
        P(),
        P("fsdp", "ctx", None),
        P("fsdp", "ctx", None),
        P("ctx", "fsdp", None),
        P("ctx", "fsdp", None),
    )
    out_specs = (P("fsdp", "ctx", None), P("fsdp", "ctx", None))
    return jax.shard_map(
        per_device, mesh=mesh, in_specs=in_specs, out_specs=out_specs, check_vma=False
    )
```
